256 devices in a mesh: grp: 16 (over y, z_lo), head: 4 (over x), tile: 4 (over z_hi, core).
Axes of the slice: x: 4, y: 4, z: 8 (z_hi: 2, z_lo: 4; z = z_hi * 4 + z_lo), core: 2. Of those that a mesh axis runs over, the one named last changes fastest.
Arguments:
- query_states: bfloat16 [16, 4, 8, 24, 4096], P('grp', None, 'tile', 'head'), may hold values from -8 to 8
- key_states: bfloat16 [16, 4, 8, 24, 4096], P('grp', None, 'tile', 'head'), may hold values from -8 to 8
- value_states: bfloat16 [16, 4, 8, 24, 4096], P('grp', None, 'tile', 'head'), may hold values from -6 to 6
- noisy_latent: float32 [16, 4, 8, 24, 64], P('grp', None, 'tile', 'head'), may hold values from -6 to 6
- noise_level: float32 [16], P('grp'), may hold values from 0.5 to 1
- head_weight: bfloat16 [4096, 64], replicated, may hold values from -0.25 to 0.25
- inlet_weight: bfloat16 [3, 3, 3, 16, 384], replicated, may hold values from -0.3125 to 0.3125
- inlet_bias: float32 [384], replicated, may hold values from -3 to 3
- temporal_weight: bfloat16 [3, 384, 768], replicated, may hold values from -0.1875 to 0.1875
- temporal_bias: float32 [768], replicated, may hold values from -3 to 3
- spatial_weight: bfloat16 [3, 3, 384, 192], replicated, may hold values from -0.109375 to 0.109375
- spatial_bias: float32 [192], replicated, may hold values from -3 to 3
Outputs:
- clean_latent: float32 [16, 4, 8, 24, 64], P('grp', None, 'tile', 'head')
- decoded_frames: bfloat16 [16, 8, 32, 96, 192], P('grp', None, 'tile', 'head')
The draws below stay inside these ranges and needn't reach their ends.
All inputs are finite; a program needn't handle non-finite values.
Results may differ from the reference program's by a relative error of at most 0.015.
Values may be sent and summed in bfloat16 or wider, within the bound.
No kernel may reach another device: no remote copies, remote signals or barrier semaphores. Data moves between devices by JAX's collectives and lax.ppermute only.
A program may use at most 64 MiB of HBM per device.

```python
import math
import jax
import jax.numpy as jnp
from jax import lax

HD = 128
HEADS = 32
ZC = 16
CH = 384
OC = 192
CF = 4
D = 4096
LAT = 64
PH = 8
PW = 24
TOKC = 768
SPANS = 16


def draw_query_states(key, part):
    key = jax.random.fold_in(key, 41)
    array_shape = (SPANS, CF, PH, PW, D)
    values = jnp.clip(1.5 * jax.random.normal(key, array_shape, jnp.float32), -7.5, 7.5)
    return values.astype(jnp.bfloat16)


def draw_key_states(key, part):
    key = jax.random.fold_in(key, 43)
    array_shape = (SPANS, CF, PH, PW, D)
    values = jnp.clip(1.5 * jax.random.normal(key, array_shape, jnp.float32), -7.5, 7.5)
    return values.astype(jnp.bfloat16)


def block_scale(rng, dims, cuts, least, high):
    def one(position, shards_of):
        heights = jax.random.uniform(jax.random.fold_in(jax.random.fold_in(rng, 6), position), (shards_of,), jnp.float32, least / len(cuts), high / len(cuts))
        return jnp.repeat(jnp.exp(heights), dims[position] // shards_of).reshape((-1,) + (1,) * (len(dims) - position - 1))

    level = one(*cuts[0])
    for cut in cuts[1:]:
        level = level * one(*cut)
    return level


def normal_values(key, dims, scale, limit, cuts=(), kind=jnp.bfloat16):
    loudness = block_scale(key, dims, cuts, -0.22, 0.18) if cuts else 1.0
    drawn = jax.random.normal(key, dims, jnp.float32) * scale * loudness
    return jnp.minimum(jnp.maximum(drawn, -limit), limit).astype(kind)


def setup_inputs(seed: int = 0) -> dict:
    keys = jax.random.split(jax.random.key(seed), 13)
    return {
        "query_states": draw_query_states(jax.random.fold_in(keys[12], 71), 0),
        "key_states": draw_key_states(jax.random.fold_in(keys[12], 71), 0),
        "value_states": normal_values(keys[2], (SPANS, CF, PH, PW, D), 1.0, 6.0, ((0, 16), (2, 4), (3, 4))),
        "noisy_latent": normal_values(keys[3], (SPANS, CF, PH, PW, LAT), 1.0, 6.0, ((0, 16), (2, 4), (3, 4)), jnp.float32),
        "noise_level": jnp.clip(jnp.exp(math.log(1.0) - 0.6931472 * jax.random.uniform(keys[4], (SPANS,), jnp.float32) ** block_scale(keys[4], (SPANS,), ((0, 16),), -0.2, 0.2)), 0.5, 1.0),
        "head_weight": normal_values(keys[5], (D, LAT), (4 * HD) ** -0.5, 0.25),
        "inlet_weight": normal_values(keys[6], (3, 3, 3, ZC, CH), (27 * ZC) ** -0.5, 0.3125),
        "inlet_bias": normal_values(keys[7], (CH,), 0.5, 3.0, (), jnp.float32),
        "temporal_weight": normal_values(keys[8], (3, CH, 2 * CH), (3 * CH) ** -0.5, 0.1875),
        "temporal_bias": normal_values(keys[9], (2 * CH,), 0.5, 3.0, (), jnp.float32),
        "spatial_weight": normal_values(keys[10], (3, 3, CH, OC), (9 * CH) ** -0.5, 0.109375),
        "spatial_bias": normal_values(keys[11], (OC,), 0.5, 3.0, (), jnp.float32),
    }


def attend_head(query_head, key_head, value_head, penalty):
    scores = jnp.dot(query_head, key_head.T, preferred_element_type=jnp.float32) * (1.0 / math.sqrt(HD))
    scores = scores + penalty[None, :]
    row_max = lax.optimization_barrier(jnp.max(scores, axis=-1, keepdims=True))
    weights = jnp.exp(scores - row_max)
    row_total = lax.optimization_barrier(jnp.sum(weights, axis=-1))
    mixture = jnp.dot(weights.astype(jnp.bfloat16), value_head, preferred_element_type=jnp.float32)
    return (mixture / row_total[:, None]).astype(jnp.bfloat16)

def inlet_filter(padded, filter_weight, filter_bias, frames_out):
    out_rows = padded.shape[1] - 2
    out_cols = padded.shape[2] - 2
    pieces = []
    for frame_shift in range(3):
        for row_shift in range(3):
            for column_shift in range(3):
                pieces.append(padded[frame_shift:frame_shift + frames_out, row_shift:row_shift + out_rows, column_shift:column_shift + out_cols, :])
    stacked = jnp.concatenate(pieces, axis=-1)
    channels = filter_weight.shape[-1]
    flat = jnp.dot(stacked.reshape(-1, stacked.shape[-1]), filter_weight.reshape(-1, channels), preferred_element_type=jnp.float32)
    return flat.reshape(frames_out, out_rows, out_cols, channels) + filter_bias

def temporal_filter(features, filter_weight, filter_bias, frames_out):
    stacked = jnp.concatenate([features[offset:offset + frames_out] for offset in range(3)], axis=-1)
    channels = features.shape[-1]
    flat = jnp.dot(stacked.reshape(-1, 3 * channels), filter_weight.reshape(3 * channels, 2 * channels), preferred_element_type=jnp.float32)
    flat = (flat + filter_bias).astype(jnp.bfloat16)
    grid_rows = features.shape[1]
    grid_cols = features.shape[2]
    split = flat.reshape(frames_out, grid_rows, grid_cols, 2, channels).transpose(0, 3, 1, 2, 4)
    return split.reshape(2 * frames_out, grid_rows, grid_cols, channels)

def spatial_filter(bordered, filter_weight, filter_bias):
    frames = bordered.shape[0]
    grid_rows = bordered.shape[1]
    grid_cols = bordered.shape[2]
    channels = bordered.shape[3]
    widened = jnp.broadcast_to(bordered[:, :, None, :, None, :], (frames, grid_rows, 2, grid_cols, 2, channels))
    widened = widened.reshape(frames, 2 * grid_rows, 2 * grid_cols, channels)[:, 1:-1, 1:-1, :]
    out_rows = 2 * grid_rows - 4
    out_cols = 2 * grid_cols - 4
    outputs = filter_weight.shape[-1]
    accum = jnp.zeros((frames * out_rows * out_cols, outputs), jnp.float32)
    for row_shift in range(3):
        for column_shift in range(3):
            window = widened[:, row_shift:row_shift + out_rows, column_shift:column_shift + out_cols, :]
            accum = accum + jnp.dot(window.reshape(-1, channels), filter_weight[row_shift, column_shift], preferred_element_type=jnp.float32)
    return (accum + filter_bias).astype(jnp.bfloat16).reshape(frames, out_rows, out_cols, outputs)

def reference(query_states, key_states, value_states, noisy_latent, noise_level, head_weight, inlet_weight, inlet_bias, temporal_weight, temporal_bias, spatial_weight, spatial_bias):
    flat_query = query_states.reshape(SPANS, TOKC, D)
    flat_key = key_states.reshape(SPANS, TOKC, D)
    flat_value = value_states.reshape(SPANS, TOKC, D)
    key_before = jnp.roll(flat_key, 1, axis=0)
    value_before = jnp.roll(flat_value, 1, axis=0)
    span_ids = jnp.arange(SPANS).astype(jnp.int32)
    noisy_flat = noisy_latent.reshape(SPANS, TOKC, LAT)

    def denoise(packed):
        query_span, key_span, value_span, key_prior, value_prior, noisy_span, noise_scale, span_id = packed
        key_window = jnp.concatenate([key_prior, key_span], axis=0)
        value_window = jnp.concatenate([value_prior, value_span], axis=0)
        column = jnp.arange(2 * TOKC).astype(jnp.int32)
        allowed = jnp.logical_or(column >= TOKC, span_id > 0)
        penalty = jnp.where(allowed, 0.0, -1e+30).astype(jnp.float32)
        query_heads = query_span.reshape(TOKC, HEADS, HD).transpose(1, 0, 2)
        key_heads = key_window.reshape(2 * TOKC, HEADS, HD).transpose(1, 0, 2)
        value_heads = value_window.reshape(2 * TOKC, HEADS, HD).transpose(1, 0, 2)

        def per_head(triple):
            return attend_head(triple[0], triple[1], triple[2], penalty)
        attention = lax.map(per_head, (query_heads, key_heads, value_heads))
        attention = attention.transpose(1, 0, 2).reshape(TOKC, D)
        velocity = jnp.dot(attention, head_weight, preferred_element_type=jnp.float32)
        return noisy_span - noise_scale * velocity
    clean = lax.map(denoise, (flat_query, flat_key, flat_value, key_before, value_before, noisy_flat, noise_level, span_ids))
    clean_latent = clean.reshape(SPANS, CF, PH, PW, LAT)
    latent = clean_latent.reshape(SPANS, CF, PH, PW, 2, 2, ZC).transpose(0, 1, 2, 4, 3, 5, 6)
    latent = latent.reshape(SPANS, CF, 2 * PH, 2 * PW, ZC).astype(jnp.bfloat16)
    prior_latent = jnp.concatenate([jnp.zeros((1, CF, 2 * PH, 2 * PW, ZC), jnp.bfloat16), latent[:-1]], axis=0)
    stacked_all = jnp.concatenate([prior_latent[:, CF - 4:], latent], axis=1)

    def decode(packed):
        stacked, span_id = packed
        padded = jnp.pad(stacked, ((0, 0), (1, 1), (1, 1), (0, 0)))
        features = inlet_filter(padded, inlet_weight, inlet_bias, CF + 2)
        keep = jnp.where(jnp.arange(CF + 2) >= 2, 1.0, (span_id > 0).astype(jnp.float32)).astype(jnp.float32)
        features = (features * keep[:, None, None, None]).astype(jnp.bfloat16)
        doubled = temporal_filter(features, temporal_weight, temporal_bias, CF)
        bordered = jnp.pad(doubled, ((0, 0), (1, 1), (1, 1), (0, 0)))
        return spatial_filter(bordered, spatial_weight, spatial_bias)
    decoded_frames = lax.map(decode, (stacked_all, span_ids))
    return (clean_latent, decoded_frames)
```

```python
import math

import jax
import jax.numpy as jnp
from jax import lax
from jax.experimental import pallas as pl
from jax.experimental.pallas import tpu as pltpu
from jax.sharding import PartitionSpec as P

HD = 128
ZC = 16
HEADS = 32
OWN = 48
LAT = 64
ROWS = 2 * OWN + OWN // 2
AXES = ("grp", "head", "tile")
VMEM_BYTES = 48 * 1024 * 1024


def device_id(y, pair, low, x, high, core):
    return ((y * 4 + 2 * pair + low) * 4 + x) * 4 + 2 * high + core


def pair_groups():
    groups = []
    for y in range(4):
        for pair in range(2):
            members = []
            for a in range(2):
                for x in range(4):
                    for b in range(2):
                        for core in range(2):
                            low = a if pair == 0 else 1 - a
                            high = b if pair == 0 or a == 1 else 1 - b
                            members.append(device_id(y, pair, low, x, high, core))
            groups.append(members)
    return groups


def prior_route(groups):
    return [(groups[g][k], groups[g + 1][k]) for g in range(len(groups) - 1) for k in range(HEADS)]


def prep_kernel(query_ref, key_ref, value_ref, weight_ref, out_ref):
    for h in range(HEADS):
        lanes = slice(h * HD, (h + 1) * HD)
        out_ref[h, 0:OWN, :] = query_ref[:, lanes]
        out_ref[h, OWN : 2 * OWN, :] = key_ref[:, lanes]
        folded = jnp.dot(value_ref[:, lanes], weight_ref[lanes, :], preferred_element_type=jnp.float32)
        packed = jnp.concatenate([folded[: OWN // 2], folded[OWN // 2 :]], axis=1)
        out_ref[h, 2 * OWN : ROWS, :] = packed.astype(jnp.bfloat16)


def prep(query, key, value, weight):
    return pl.pallas_call(
        prep_kernel,
        out_shape=jax.ShapeDtypeStruct((HEADS, ROWS, HD), jnp.bfloat16),
        in_specs=[pl.BlockSpec(memory_space=pltpu.VMEM)] * 4,
        out_specs=pl.BlockSpec(memory_space=pltpu.VMEM),
        compiler_params=pltpu.CompilerParams(vmem_limit_bytes=VMEM_BYTES),
    )(query, key, value, weight)


def spread_values(packed, target):
    lower = packed[:, :, :LAT].astype(jnp.float32)
    upper = packed[:, :, LAT:].astype(jnp.float32)
    both = jnp.concatenate([lower, upper], axis=1).reshape(16 * OWN, LAT)
    ones = jnp.ones((16 * OWN, HD - LAT), jnp.float32)
    target[...] = jnp.concatenate([both, ones], axis=1).astype(jnp.bfloat16)


def fold_scale():
    return (1.0 / math.sqrt(HD)) * math.log2(math.e)


def scores_of(query, keys):
    dims = (((1,), (1,)), ((), ()))
    return lax.dot_general(query, keys, dims, preferred_element_type=jnp.float32)


def pack_result(mixed, out_ref, start, blocks):
    velocity = mixed[:, :LAT] / mixed[:, LAT : 2 * LAT]
    velocity = velocity.reshape(blocks, OWN, LAT)
    packed = jnp.concatenate([velocity[:, : OWN // 2], velocity[:, OWN // 2 :]], axis=2)
    out_ref[pl.ds(start, blocks)] = packed.astype(out_ref.dtype)


QB = 4


def attend_here_kernel(place_ref, recv_ref, out_ref, max_ref, mix_ref, early_v, late_v):
    early = place_ref[0]
    late = 16 - early
    spread_values(recv_ref[pl.ds(early, 16), 2 * OWN :, :], early_v)
    spread_values(recv_ref[pl.ds(late, 16), 2 * OWN :, :], late_v)
    early_k = recv_ref[pl.ds(early, 16), OWN : 2 * OWN, :].reshape(16 * OWN, HD)
    late_k = recv_ref[pl.ds(late, 16), OWN : 2 * OWN, :].reshape(16 * OWN, HD)
    scale = fold_scale()

    def late_block(i, carry):
        query = recv_ref[pl.ds(late + i * QB, QB), :OWN, :].reshape(QB * OWN, HD)
        here = scores_of(query, late_k) * scale
        before = scores_of(query, early_k) * scale
        top = jnp.maximum(
            jnp.max(here, axis=1, keepdims=True), jnp.max(before, axis=1, keepdims=True)
        )
        here = jnp.exp2(here - top).astype(jnp.bfloat16)
        before = jnp.exp2(before - top).astype(jnp.bfloat16)
        mixed = jnp.dot(here, late_v[...], preferred_element_type=jnp.float32)
        mixed += jnp.dot(before, early_v[...], preferred_element_type=jnp.float32)
        pack_result(mixed, out_ref, i * QB, QB)
        return carry

    lax.fori_loop(0, 16 // QB, late_block, 0)

    def early_block(i, carry):
        query = recv_ref[pl.ds(early + i * QB, QB), :OWN, :].reshape(QB * OWN, HD)
        here = scores_of(query, early_k) * scale
        top = jnp.max(here, axis=1, keepdims=True)
        here = jnp.exp2(here - top).astype(jnp.bfloat16)
        mix_ref[pl.ds(i * QB * OWN, QB * OWN), :] = jnp.dot(
            here, early_v[...], preferred_element_type=jnp.float32
        )
        max_ref[pl.ds(i * QB * OWN, QB * OWN), :] = jnp.broadcast_to(top, (QB * OWN, HD))
        return carry

    lax.fori_loop(0, 16 // QB, early_block, 0)


def attend_here(place, recv):
    vmem = pl.BlockSpec(memory_space=pltpu.VMEM)
    tokens = 16 * OWN
    return pl.pallas_call(
        attend_here_kernel,
        out_shape=(
            jax.ShapeDtypeStruct((16, OWN // 2, HD), jnp.bfloat16),
            jax.ShapeDtypeStruct((tokens, HD), jnp.float32),
            jax.ShapeDtypeStruct((tokens, HD), jnp.float32),
        ),
        in_specs=[pl.BlockSpec(memory_space=pltpu.SMEM), vmem],
        out_specs=(vmem, vmem, vmem),
        scratch_shapes=[pltpu.VMEM((tokens, HD), jnp.bfloat16)] * 2,
        compiler_params=pltpu.CompilerParams(vmem_limit_bytes=VMEM_BYTES),
        cost_estimate=pl.CostEstimate(
            flops=4 * 3 * tokens * tokens * HD, bytes_accessed=4 << 20, transcendentals=3 * tokens * tokens
        ),
    )(place, recv)


def attend_prior_kernel(place_ref, recv_ref, prior_ref, late_ref, max_ref, mix_ref, out_ref, prior_v):
    early = place_ref[0]
    late = 16 - early
    penalty = jnp.where(place_ref[1] > 0, 0.0, -1e30).astype(jnp.float32)
    spread_values(prior_ref[:, OWN:, :], prior_v)
    prior_k = prior_ref[:, :OWN, :].reshape(16 * OWN, HD)
    scale = fold_scale()
    out_ref[pl.ds(late, 16)] = late_ref[...]

    def block(i, carry):
        rows = pl.ds(i * QB * OWN, QB * OWN)
        query = recv_ref[pl.ds(early + i * QB, QB), :OWN, :].reshape(QB * OWN, HD)
        before = scores_of(query, prior_k) * scale + penalty
        old = max_ref[rows, :]
        top = jnp.maximum(old[:, :1], jnp.max(before, axis=1, keepdims=True))
        before = jnp.exp2(before - top).astype(jnp.bfloat16)
        mixed = jnp.dot(before, prior_v[...], preferred_element_type=jnp.float32)
        mixed += mix_ref[rows, :] * jnp.exp2(old - top)
        pack_result(mixed, out_ref, early + i * QB, QB)
        return carry

    lax.fori_loop(0, 16 // QB, block, 0)


def attend_prior(place, recv, prior, late, top, mix):
    vmem = pl.BlockSpec(memory_space=pltpu.VMEM)
    tokens = 16 * OWN
    return pl.pallas_call(
        attend_prior_kernel,
        out_shape=jax.ShapeDtypeStruct((HEADS, OWN // 2, HD), jnp.bfloat16),
        in_specs=[pl.BlockSpec(memory_space=pltpu.SMEM)] + [vmem] * 5,
        out_specs=vmem,
        scratch_shapes=[pltpu.VMEM((tokens, HD), jnp.bfloat16)],
        compiler_params=pltpu.CompilerParams(vmem_limit_bytes=VMEM_BYTES),
    )(place, recv, prior, late, top, mix)


def shifted(block, axis, distance):
    devices = range(lax.axis_size(axis))
    route = [(i - distance, i) for i in devices if i - distance in devices]
    return lax.ppermute(block, axis, route)


def with_halo(cells, sides, width):
    for axis, dim in sides:
        count = lax.axis_size(axis)
        ends = count - 1
        head = lax.slice_in_dim(cells, 0, width, axis=dim)
        tail = lax.slice_in_dim(cells, cells.shape[dim] - width, cells.shape[dim], axis=dim)
        cells = jnp.concatenate(
            [
                lax.ppermute(tail, axis, [(i, (i + 1) % count) for i in range(ends)]),
                cells,
                lax.ppermute(head, axis, [((i + 1) % count, i) for i in range(ends)]),
            ],
            axis=dim,
        )
    return cells


def inlet_filter(padded, filter_weight, filter_bias, frames_out):
    out_rows = padded.shape[1] - 2
    out_cols = padded.shape[2] - 2
    pieces = []
    for frame_shift in range(3):
        for row_shift in range(3):
            for column_shift in range(3):
                pieces.append(
                    padded[
                        frame_shift : frame_shift + frames_out,
                        row_shift : row_shift + out_rows,
                        column_shift : column_shift + out_cols,
                        :,
                    ]
                )
    stacked = jnp.concatenate(pieces, axis=-1)
    channels = filter_weight.shape[-1]
    flat = jnp.dot(
        stacked.reshape(-1, stacked.shape[-1]),
        filter_weight.reshape(-1, channels),
        preferred_element_type=jnp.float32,
    )
    return flat.reshape(frames_out, out_rows, out_cols, channels) + filter_bias


def temporal_filter(features, filter_weight, filter_bias, frames_out):
    stacked = jnp.concatenate(
        [features[offset : offset + frames_out] for offset in range(3)], axis=-1
    )
    channels = features.shape[-1]
    flat = jnp.dot(
        stacked.reshape(-1, 3 * channels),
        filter_weight.reshape(3 * channels, 2 * channels),
        preferred_element_type=jnp.float32,
    )
    flat = (flat + filter_bias).astype(jnp.bfloat16)
    grid_rows = features.shape[1]
    grid_cols = features.shape[2]
    split = flat.reshape(frames_out, grid_rows, grid_cols, 2, channels).transpose(0, 3, 1, 2, 4)
    return split.reshape(2 * frames_out, grid_rows, grid_cols, channels)


def spatial_filter(bordered, filter_weight, filter_bias):
    frames = bordered.shape[0]
    grid_rows = bordered.shape[1]
    grid_cols = bordered.shape[2]
    channels = bordered.shape[3]
    widened = jnp.broadcast_to(
        bordered[:, :, None, :, None, :], (frames, grid_rows, 2, grid_cols, 2, channels)
    )
    widened = widened.reshape(frames, 2 * grid_rows, 2 * grid_cols, channels)[:, 1:-1, 1:-1, :]
    out_rows = 2 * grid_rows - 4
    out_cols = 2 * grid_cols - 4
    outputs = filter_weight.shape[-1]
    accum = jnp.zeros((frames * out_rows * out_cols, outputs), jnp.float32)
    for row_shift in range(3):
        for column_shift in range(3):
            window = widened[
                :, row_shift : row_shift + out_rows, column_shift : column_shift + out_cols, :
            ]
            accum = accum + jnp.dot(
                window.reshape(-1, channels),
                filter_weight[row_shift, column_shift],
                preferred_element_type=jnp.float32,
            )
    return (accum + filter_bias).astype(jnp.bfloat16).reshape(frames, out_rows, out_cols, outputs)


def shards(
    query_states,
    key_states,
    value_states,
    noisy_latent,
    noise_level,
    head_weight,
    inlet_weight,
    inlet_bias,
    temporal_weight,
    temporal_bias,
    spatial_weight,
    spatial_bias,
):
    frames_span = query_states.shape[1]
    patch_rows = query_states.shape[2]
    patch_cols = query_states.shape[3]
    model_width = query_states.shape[4]
    groups = pair_groups()
    grp = lax.axis_index("grp")
    pair = (grp // 2) % 2
    has_prior = grp > 0
    early = 16 * pair
    pair_has_prior = (grp // 2 > 0).astype(jnp.int32)
    place = jnp.stack([early.astype(jnp.int32), pair_has_prior])
    sent = prep(
        query_states.reshape(-1, model_width),
        key_states.reshape(-1, model_width),
        value_states.reshape(-1, model_width),
        head_weight,
    )
    recv = lax.all_to_all(sent, AXES, 0, 0, tiled=True, axis_index_groups=groups)
    late_kv = lax.dynamic_slice(recv, (16 - early, OWN, 0), (16, ROWS - OWN, HD))
    prior = lax.ppermute(late_kv, AXES, prior_route(groups))
    late, top, mix = attend_here(place, recv)
    partial = attend_prior(place, recv, prior, late, top, mix)
    back = lax.all_to_all(partial, AXES, 0, 0, tiled=True, axis_index_groups=groups)
    packed = jnp.sum(back.astype(jnp.float32), axis=0)
    velocity = jnp.concatenate([packed[:, :LAT], packed[:, LAT:]], axis=0)
    noisy_flat = noisy_latent.reshape(-1, noisy_latent.shape[-1])
    clean_flat = noisy_flat - noise_level[0] * velocity
    clean_latent = clean_flat.reshape(noisy_latent.shape)
    latent_tile = clean_flat.reshape(frames_span, patch_rows, patch_cols, 2, 2, ZC).transpose(
        0, 1, 3, 2, 4, 5
    )
    latent_tile = latent_tile.reshape(frames_span, 2 * patch_rows, 2 * patch_cols, ZC).astype(
        jnp.bfloat16
    )
    prior_tile = shifted(latent_tile, "grp", 1)
    stacked = jnp.concatenate([prior_tile, latent_tile], axis=0)
    tile_rows = 2 * patch_rows
    tile_cols = 2 * patch_cols
    prior_keep = jnp.where(jnp.arange(frames_span + 2) >= 2, 1.0, has_prior.astype(jnp.float32))
    padded = with_halo(stacked, (("head", 2), ("tile", 1)), 2)
    features = inlet_filter(padded, inlet_weight, inlet_bias, frames_span + 2)
    row_global = lax.axis_index("tile") * tile_rows + jnp.arange(tile_rows + 2) - 1
    column_global = lax.axis_index("head") * tile_cols + jnp.arange(tile_cols + 2) - 1
    row_inside = jnp.logical_and(row_global >= 0, row_global < tile_rows * lax.axis_size("tile"))
    column_inside = jnp.logical_and(
        column_global >= 0, column_global < tile_cols * lax.axis_size("head")
    )
    inside = jnp.logical_and(row_inside[:, None], column_inside[None, :]).astype(jnp.float32)
    features = (features * prior_keep[:, None, None, None] * inside[None, :, :, None]).astype(
        jnp.bfloat16
    )
    doubled = temporal_filter(features, temporal_weight, temporal_bias, frames_span)
    bordered = doubled * inside[None, :, :, None].astype(jnp.bfloat16)
    decoded = spatial_filter(bordered, spatial_weight, spatial_bias)
    return (clean_latent, decoded[None])


def solution(mesh):
    return jax.shard_map(
        shards,
        mesh=mesh,
        in_specs=(
            P("grp", None, "tile", "head", None),
            P("grp", None, "tile", "head", None),
            P("grp", None, "tile", "head", None),
            P("grp", None, "tile", "head", None),
            P("grp"),
            P(),
            P(),
            P(),
            P(),
            P(),
            P(),
            P(),
        ),
        out_specs=(P("grp", None, "tile", "head", None), P("grp", None, "tile", "head", None)),
        check_vma=False,
    )
```

```python
import math

import jax
import jax.numpy as jnp
from jax import lax
from jax.experimental import pallas as pl
from jax.experimental.pallas import tpu as pltpu
from jax.sharding import PartitionSpec as P

HD = 128
ZC = 16
HEADS = 32
OWN = 48
LAT = 64
ROWS = 2 * OWN + OWN // 2
AXES = ("grp", "head", "tile")
VMEM_BYTES = 32 * 1024 * 1024


def device_id(y, pair, low, x, high, core):
    return ((y * 4 + 2 * pair + low) * 4 + x) * 4 + 2 * high + core


def pair_groups():
    groups = []
    for y in range(4):
        for pair in range(2):
            members = []
            for a in range(2):
                for x in range(4):
                    for b in range(2):
                        for core in range(2):
                            low = a if pair == 0 else 1 - a
                            high = b if pair == 0 or a == 1 else 1 - b
                            members.append(device_id(y, pair, low, x, high, core))
            groups.append(members)
    return groups


def half_groups(groups):
    return [[d for d in group if d // 2 % 2 == high] for group in groups for high in range(2)]


def prior_route(groups):
    return [(groups[g][k], groups[g + 1][k]) for g in range(len(groups) - 1) for k in range(HEADS)]


PREP_STEPS = 4
PREP_HEADS = HEADS // PREP_STEPS


def prep_kernel(query_ref, key_ref, value_ref, weight_ref, out_ref):
    dims = (((1,), (1,)), ((), ()))
    for h in range(PREP_HEADS):
        lanes = slice(h * HD, (h + 1) * HD)
        out_ref[h, 0:OWN, :] = query_ref[:, lanes]
        out_ref[h, OWN : 2 * OWN, :] = key_ref[:, lanes]
        folded = lax.dot_general(
            value_ref[:, lanes], weight_ref[:, lanes], dims, preferred_element_type=jnp.float32
        )
        packed = jnp.concatenate([folded[: OWN // 2], folded[OWN // 2 :]], axis=1)
        out_ref[h, 2 * OWN : ROWS, :] = packed.astype(jnp.bfloat16)


def token_rows(states):
    return states.transpose(0, 1, 3, 2, 4).reshape(OWN, states.shape[-1])


def prep(query, key, value, weight):
    width = PREP_HEADS * HD
    tile = pl.BlockSpec((OWN, width), lambda i: (0, i))
    return pl.pallas_call(
        prep_kernel,
        grid=(PREP_STEPS,),
        out_shape=jax.ShapeDtypeStruct((HEADS, ROWS, HD), jnp.bfloat16),
        in_specs=[tile, tile, tile, pl.BlockSpec((LAT, width), lambda i: (0, i))],
        out_specs=pl.BlockSpec((PREP_HEADS, ROWS, HD), lambda i: (i, 0, 0)),
        compiler_params=pltpu.CompilerParams(vmem_limit_bytes=16 * 1024 * 1024),
    )(token_rows(query), token_rows(key), token_rows(value), weight.T)


def spread_values(packed, target):
    lower = packed[:, :, :LAT].astype(jnp.float32)
    upper = packed[:, :, LAT:].astype(jnp.float32)
    both = jnp.concatenate([lower, upper], axis=1).reshape(16 * OWN, LAT)
    ones = jnp.ones((16 * OWN, HD - LAT), jnp.float32)
    target[...] = jnp.concatenate([both, ones], axis=1).astype(jnp.bfloat16)


def fold_scale():
    return (1.0 / math.sqrt(HD)) * math.log2(math.e)


def scores_of(query, keys):
    dims = (((1,), (1,)), ((), ()))
    return lax.dot_general(query, keys, dims, preferred_element_type=jnp.float32)


def pack_result(mixed, out_ref, start, blocks):
    velocity = mixed[:, :LAT] / mixed[:, LAT : 2 * LAT]
    velocity = velocity.reshape(blocks, OWN, LAT)
    packed = jnp.concatenate([velocity[:, : OWN // 2], velocity[:, OWN // 2 :]], axis=2)
    out_ref[pl.ds(start, blocks)] = packed.astype(out_ref.dtype)


QB = 16
PB = 8


def late_part_kernel(place_ref, recv_ref, *rest):
    rest[-1][...] = recv_ref[pl.ds(16 - place_ref[0], 16), OWN:, :]


def late_part(place, recv, ready):
    vmem = pl.BlockSpec(memory_space=pltpu.VMEM)
    return pl.pallas_call(
        late_part_kernel,
        out_shape=jax.ShapeDtypeStruct((16, ROWS - OWN, HD), jnp.bfloat16),
        in_specs=[pl.BlockSpec(memory_space=pltpu.SMEM), vmem]
        + [pl.BlockSpec(memory_space=pl.ANY)] * len(ready),
        out_specs=vmem,
        compiler_params=pltpu.CompilerParams(vmem_limit_bytes=4 * 1024 * 1024),
    )(place, recv, *ready)


def attend_here_kernel(place_ref, recv_ref, out_ref, max_ref, mix_ref, early_v, late_v):
    early = place_ref[0]
    late = 16 - early
    spread_values(recv_ref[pl.ds(early, 16), 2 * OWN :, :], early_v)
    spread_values(recv_ref[pl.ds(late, 16), 2 * OWN :, :], late_v)
    early_k = recv_ref[pl.ds(early, 16), OWN : 2 * OWN, :].reshape(16 * OWN, HD)
    late_k = recv_ref[pl.ds(late, 16), OWN : 2 * OWN, :].reshape(16 * OWN, HD)
    scale = fold_scale()

    def late_block(i, carry):
        query = recv_ref[pl.ds(late + i * QB, QB), :OWN, :].reshape(QB * OWN, HD)
        here = scores_of(query, late_k) * scale
        before = scores_of(query, early_k) * scale
        top = jnp.maximum(
            jnp.max(here, axis=1, keepdims=True), jnp.max(before, axis=1, keepdims=True)
        )
        here = jnp.exp2(here - top).astype(jnp.bfloat16)
        before = jnp.exp2(before - top).astype(jnp.bfloat16)
        mixed = jnp.dot(here, late_v[...], preferred_element_type=jnp.float32)
        mixed += jnp.dot(before, early_v[...], preferred_element_type=jnp.float32)
        pack_result(mixed, out_ref, i * QB, QB)
        return carry

    lax.fori_loop(0, 16 // QB, late_block, 0)

    def early_block(i, carry):
        query = recv_ref[pl.ds(early + i * QB, QB), :OWN, :].reshape(QB * OWN, HD)
        here = scores_of(query, early_k) * scale
        top = jnp.max(here, axis=1, keepdims=True)
        here = jnp.exp2(here - top).astype(jnp.bfloat16)
        mix_ref[pl.ds(i * QB * OWN, QB * OWN), :] = jnp.dot(
            here, early_v[...], preferred_element_type=jnp.float32
        )
        max_ref[pl.ds(i * QB * OWN, QB * OWN), :] = jnp.broadcast_to(top, (QB * OWN, HD))
        return carry

    lax.fori_loop(0, 16 // QB, early_block, 0)


def attend_here(place, recv):
    vmem = pl.BlockSpec(memory_space=pltpu.VMEM)
    tokens = 16 * OWN
    return pl.pallas_call(
        attend_here_kernel,
        out_shape=(
            jax.ShapeDtypeStruct((16, OWN // 2, HD), jnp.float32),
            jax.ShapeDtypeStruct((tokens, HD), jnp.float32),
            jax.ShapeDtypeStruct((tokens, HD), jnp.float32),
        ),
        in_specs=[pl.BlockSpec(memory_space=pltpu.SMEM), vmem],
        out_specs=(vmem, vmem, vmem),
        scratch_shapes=[pltpu.VMEM((tokens, HD), jnp.bfloat16)] * 2,
        compiler_params=pltpu.CompilerParams(vmem_limit_bytes=VMEM_BYTES),
        cost_estimate=pl.CostEstimate(
            flops=4 * 3 * tokens * tokens * HD, bytes_accessed=4 << 20, transcendentals=3 * tokens * tokens
        ),
    )(place, recv)


def attend_prior_kernel(
    place_ref, recv_ref, prior_ref, late_ref, max_ref, mix_ref, out_hbm, prior_v, packed_ref, grid_ref,
    out_ref, sem,
):
    early = place_ref[0]
    late = 16 - early
    penalty = jnp.where(place_ref[1] > 0, 0.0, -1e30).astype(jnp.float32)
    spread_values(prior_ref[:, OWN:, :], prior_v)
    prior_k = prior_ref[:, :OWN, :].reshape(16 * OWN, HD)
    scale = fold_scale()
    packed_ref[pl.ds(late, 16)] = late_ref[...]

    def block(i, carry):
        rows = pl.ds(i * PB * OWN, PB * OWN)
        query = recv_ref[pl.ds(early + i * PB, PB), :OWN, :].reshape(PB * OWN, HD)
        before = scores_of(query, prior_k) * scale + penalty
        old = max_ref[rows, :]
        top = jnp.maximum(old[:, :1], jnp.max(before, axis=1, keepdims=True))
        before = jnp.exp2(before - top).astype(jnp.bfloat16)
        mixed = jnp.dot(before, prior_v[...], preferred_element_type=jnp.float32)
        mixed += mix_ref[rows, :] * jnp.exp2(old - top)
        pack_result(mixed, packed_ref, early + i * PB, PB)
        return carry

    lax.fori_loop(0, 16 // PB, block, 0, unroll=True)
    scatter_halo(place_ref, packed_ref, grid_ref, out_ref)
    copy = pltpu.make_async_copy(out_ref, out_hbm, sem)
    copy.start()
    copy.wait()


def scatter_halo(place_ref, packed_ref, grid_ref, out_ref):
    flip = place_ref[2]
    high = place_ref[3]
    grid_ref[...] = jnp.zeros_like(grid_ref)
    for a in range(2):
        for b in range(2):
            tile_high = b if a == 1 else jnp.where(flip > 0, 1 - b, b)
            for core in range(2):
                row = 2 * (2 * tile_high + core) + 1
                for x in range(4):
                    block = a * 16 + x * 4 + b * 2 + core
                    for frame in range(2):
                        for sub in range(2):
                            line = packed_ref[block, pl.ds(frame * 12 + sub, 6, stride=2), :]
                            grid_ref[a, x, frame, row + sub, 1:7, :] = line
                            if x < 3:
                                grid_ref[a, x + 1, frame, row + sub, 0:1, :] = line[5:6]
                            if x > 0:
                                grid_ref[a, x - 1, frame, row + sub, 7:8, :] = line[0:1]
    for a in range(2):
        for x in range(4):
            for core in range(2):
                for part in range(2):
                    row = 2 * (2 * (high if part == 0 else 1 - high) + core)
                    tile = grid_ref[a, x, :, pl.ds(row, 4), :, :].reshape(64, HD)
                    out_ref[a * 8 + x * 2 + core, part * 64 : (part + 1) * 64, :] = tile.astype(
                        jnp.bfloat16
                    )


def attend_prior(place, recv, prior, late, top, mix):
    vmem = pl.BlockSpec(memory_space=pltpu.VMEM)
    tokens = 16 * OWN
    return pl.pallas_call(
        attend_prior_kernel,
        out_shape=pltpu.HBM((16, 128, HD), jnp.bfloat16),
        in_specs=[pl.BlockSpec(memory_space=pltpu.SMEM)] + [vmem] * 5,
        out_specs=pl.BlockSpec(memory_space=pltpu.HBM),
        scratch_shapes=[
            pltpu.VMEM((tokens, HD), jnp.bfloat16),
            pltpu.VMEM((HEADS, OWN // 2, HD), jnp.float32),
            pltpu.VMEM((2, 4, 2, 10, 8, HD), jnp.float32),
            pltpu.VMEM((16, 128, HD), jnp.bfloat16),
            pltpu.SemaphoreType.DMA,
        ],
        compiler_params=pltpu.CompilerParams(vmem_limit_bytes=VMEM_BYTES),
    )(place, recv, prior, late, top, mix)


def sum_kernel(back_ref, own_ref, other_ref):
    total = back_ref[0].astype(jnp.float32)
    for k in range(1, 16):
        total += back_ref[k].astype(jnp.float32)
    own_ref[...] = total[:64]
    other_ref[...] = total[64:].astype(jnp.bfloat16)


def sum_heads(back):
    vmem = pl.BlockSpec(memory_space=pltpu.VMEM)
    return pl.pallas_call(
        sum_kernel,
        out_shape=(
            jax.ShapeDtypeStruct((64, HD), jnp.float32),
            jax.ShapeDtypeStruct((64, HD), jnp.bfloat16),
        ),
        in_specs=[vmem],
        out_specs=(vmem, vmem),
        compiler_params=pltpu.CompilerParams(vmem_limit_bytes=4 * 1024 * 1024),
    )(back)


CH = 384
OC = 192
TAPS = {(0, 0): (0, 1), (0, 1): (2,), (1, 0): (0,), (1, 1): (1, 2)}


def spread_inlet(inlet_ref, wide_ref):
    wide_ref[...] = jnp.zeros_like(wide_ref)
    for frame in range(3):
        for b in range(3):
            for e in range(3):
                tap = inlet_ref[((frame * 3 + b) * 3 + e) * ZC : ((frame * 3 + b) * 3 + e + 1) * ZC, :]
                for down in range(2):
                    for right in range(2):
                        u, v = b + down, e + right
                        row = frame * 256 + (u // 2 * 2 + v // 2) * LAT + (u % 2 * 2 + v % 2) * ZC
                        sub = 2 * down + right
                        wide_ref[row : row + ZC, sub * CH : (sub + 1) * CH] = tap


def window_kernel(spatial_ref, window_ref):
    for wy in range(2):
        for wx in range(2):
            rows = slice((2 * wy + wx) * CH, (2 * wy + wx + 1) * CH)
            rest = []
            for oy in range(2):
                for ox in range(2):
                    total = None
                    for b in TAPS[oy, wy]:
                        for e in TAPS[ox, wx]:
                            tap = spatial_ref[b, e].astype(jnp.float32)
                            total = tap if total is None else total + tap
                    out = 2 * oy + ox
                    window_ref[rows, out * 128 : (out + 1) * 128] = total[:, :128].astype(jnp.bfloat16)
                    rest.append(total[:, 128:])
            for oy in range(2):
                both = jnp.concatenate([rest[2 * oy], rest[2 * oy + 1]], axis=1)
                window_ref[rows, (4 + oy) * 128 : (5 + oy) * 128] = both.astype(jnp.bfloat16)


def window_weights(spatial_weight):
    vmem = pl.BlockSpec(memory_space=pltpu.VMEM)
    return pl.pallas_call(
        window_kernel,
        out_shape=jax.ShapeDtypeStruct((4 * CH, 4 * OC), jnp.bfloat16),
        in_specs=[vmem],
        out_specs=vmem,
        compiler_params=pltpu.CompilerParams(vmem_limit_bytes=16 * 1024 * 1024),
        cost_estimate=pl.CostEstimate(flops=4 << 20, bytes_accessed=4 << 20, transcendentals=0),
    )(spatial_weight)


WIN = 24


def decode_kernel(
    place_ref, before_ref, now_ref, inlet_ref, inlet_bias_ref, time_hbm, time_bias_ref, window_hbm,
    space_bias_ref, out_ref, patch_ref, feature_ref, time_in_ref, double_ref, shift_ref, space_in_ref,
    low_ref, rest_ref, wide_ref, time_ref, window_ref, sems,
):
    time_copy = pltpu.make_async_copy(time_hbm, time_ref, sems.at[0])
    time_copy.start()
    window_copy = pltpu.make_async_copy(window_hbm, window_ref, sems.at[1])
    window_copy.start()
    has_prior, tile, head = place_ref[0], place_ref[1], place_ref[2]
    spread_inlet(inlet_ref, wide_ref)
    for half, ref in enumerate((before_ref, now_ref)):
        cells = ref[...].astype(jnp.float32)
        after = jnp.concatenate([cells[1:], cells[:1]], axis=0)
        for part in range(2):
            lanes = slice(part * LAT, (part + 1) * LAT)
            pairs = jnp.concatenate([cells[:, lanes], after[:, lanes]], axis=1)
            for frame in range(2):
                row = (half * 4 + part * 2 + frame) * WIN
                patch_ref[row : row + WIN, :128] = pairs[frame * 32 : frame * 32 + WIN]
                patch_ref[row : row + WIN, 128:] = pairs[frame * 32 + 8 : frame * 32 + 8 + WIN]
    taps = [patch_ref[a * WIN : (a + 6) * WIN, :].astype(jnp.bfloat16) for a in range(3)]
    features = jnp.dot(
        jnp.concatenate(taps, axis=1), wide_ref[...], preferred_element_type=jnp.float32
    )
    frame_row = lax.broadcasted_iota(jnp.int32, (6 * WIN, 1), 0)
    keep = jnp.logical_or(frame_row >= 2 * WIN, has_prior > 0)
    for sub in range(4):
        lanes = slice(sub * CH, (sub + 1) * CH)
        value = jnp.where(keep, features[:, lanes] + inlet_bias_ref[...], 0.0)
        feature_ref[:, lanes] = value
    for sub in range(4):
        for a in range(3):
            time_in_ref[sub * 96 : (sub + 1) * 96, a * CH : (a + 1) * CH] = feature_ref[
                a * WIN : a * WIN + 96, sub * CH : (sub + 1) * CH
            ].astype(jnp.bfloat16)
    time_copy.wait()
    doubled = jnp.dot(time_in_ref[...], time_ref[...], preferred_element_type=jnp.float32)
    place = lax.broadcasted_iota(jnp.int32, (96, 1), 0)
    window_row = lax.rem(place, WIN) // 8
    window_col = lax.rem(place, 8)
    for sub in range(4):
        row = 4 * tile + 2 * window_row - 1 + sub // 2
        col = 12 * head + 2 * window_col - 1 + sub % 2
        inside = jnp.logical_and(
            jnp.logical_and(row >= 0, row < 16), jnp.logical_and(col >= 0, col < 48)
        )
        value = jnp.where(inside, doubled[sub * 96 : (sub + 1) * 96] + time_bias_ref[...], 0.0)
        double_ref[sub, :96, :] = value
        double_ref[sub, 96:, :] = jnp.zeros((16, 2 * CH), jnp.float32)
        if sub % 2 == 0:
            shift_ref[sub // 2, :103, :] = double_ref[sub, 1:104, :]
            shift_ref[sub // 2, 103:, :] = jnp.zeros((9, 2 * CH), jnp.float32)
    for py in range(2):
        for px in range(2):
            for wy in range(2):
                for wx in range(2):
                    down, right = (py + wy) // 2, (px + wx) // 2
                    alpha, beta = (py + wy) % 2, (px + wx) % 2
                    for u in range(2):
                        lanes = slice(u * CH, (u + 1) * CH)
                        rows = slice(down * 8, down * 8 + 96)
                        if right:
                            value = shift_ref[alpha, rows, lanes]
                        else:
                            value = double_ref[2 * alpha + beta, rows, lanes]
                        start = ((2 * py + px) * 2 + u) * 96
                        piece = (2 * wy + wx) * CH
                        space_in_ref[start : start + 96, piece : piece + CH] = value.astype(
                            jnp.bfloat16
                        )
    window_copy.wait()
    for py in range(2):
        for px in range(2):
            start = (2 * py + px) * 192
            mixed = jnp.dot(
                space_in_ref[start : start + 192, :], window_ref[...], preferred_element_type=jnp.float32
            )
            for oy in range(2):
                for ox in range(2):
                    column = 8 - 1 + 2 * px + ox
                    out = 2 * oy + ox
                    for ri in range(3):
                        high = 4 * ri - 1 + 2 * py + oy
                        if not 0 <= high < 8:
                            continue
                        for u in range(2):
                            for t in range(4):
                                row = u * 96 + t * WIN + ri * 8
                                low = mixed[row : row + 8, out * 128 : (out + 1) * 128]
                                rest = mixed[row : row + 8, (4 + oy) * 128 : (5 + oy) * 128]
                                if ox:
                                    rest = pltpu.roll(rest, 64, 1)
                                spot = pl.ds(column, 8, stride=4)
                                low_ref[(2 * t + u) * 8 + high, spot, :] = low
                                rest_ref[(2 * t + u) * 8 + high, spot, :] = rest
    low_bias = space_bias_ref[:, :128]
    rest_bias = space_bias_ref[:, 128:]
    for frame in range(8):
        for high in range(8):
            line = frame * 8 + high
            out_ref[frame, high, :, :128] = (low_ref[line, 8:32, :] + low_bias).astype(jnp.bfloat16)
            out_ref[frame, high, :, 128:] = (rest_ref[line, 8:32, :LAT] + rest_bias).astype(
                jnp.bfloat16
            )


def decode(place, before, now, inlet, inlet_bias, time_weight, time_bias, window, space_bias):
    vmem = pl.BlockSpec(memory_space=pltpu.VMEM)
    hbm = pl.BlockSpec(memory_space=pltpu.HBM)
    f32, bf16 = jnp.float32, jnp.bfloat16
    time_weight = pltpu.with_memory_space_constraint(time_weight, pltpu.HBM)
    window = pltpu.with_memory_space_constraint(window, pltpu.HBM)
    return pl.pallas_call(
        decode_kernel,
        out_shape=jax.ShapeDtypeStruct((8, 8, 24, OC), bf16),
        in_specs=[pl.BlockSpec(memory_space=pltpu.SMEM)] + [vmem] * 4 + [hbm, vmem, hbm, vmem],
        out_specs=vmem,
        scratch_shapes=[
            pltpu.VMEM((8 * WIN, 256), f32),
            pltpu.VMEM((6 * WIN, 4 * CH), f32),
            pltpu.VMEM((384, 3 * CH), bf16),
            pltpu.VMEM((4, 112, 2 * CH), f32),
            pltpu.VMEM((2, 112, 2 * CH), f32),
            pltpu.VMEM((768, 4 * CH), bf16),
            pltpu.VMEM((64, 40, 128), f32),
            pltpu.VMEM((64, 40, 128), f32),
            pltpu.VMEM((768, 4 * CH), bf16),
            pltpu.VMEM((3 * CH, 2 * CH), bf16),
            pltpu.VMEM((4 * CH, 4 * OC), bf16),
            pltpu.SemaphoreType.DMA((2,)),
        ],
        compiler_params=pltpu.CompilerParams(vmem_limit_bytes=VMEM_BYTES),
    )(place, before, now, inlet, inlet_bias, time_weight, time_bias, window, space_bias)


def shifted(block, axis, distance):
    devices = range(lax.axis_size(axis))
    route = [(i - distance, i) for i in devices if i - distance in devices]
    return lax.ppermute(block, axis, route)


def with_halo(cells, sides, width):
    for axis, dim in sides:
        count = lax.axis_size(axis)
        ends = count - 1
        head = lax.slice_in_dim(cells, 0, width, axis=dim)
        tail = lax.slice_in_dim(cells, cells.shape[dim] - width, cells.shape[dim], axis=dim)
        cells = jnp.concatenate(
            [
                lax.ppermute(tail, axis, [(i, (i + 1) % count) for i in range(ends)]),
                cells,
                lax.ppermute(head, axis, [((i + 1) % count, i) for i in range(ends)]),
            ],
            axis=dim,
        )
    return cells


def shards(
    query_states,
    key_states,
    value_states,
    noisy_latent,
    noise_level,
    head_weight,
    inlet_weight,
    inlet_bias,
    temporal_weight,
    temporal_bias,
    spatial_weight,
    spatial_bias,
):
    groups = pair_groups()
    grp = lax.axis_index("grp")
    pair = (grp // 2) % 2
    has_prior = grp > 0
    early = 16 * pair
    pair_has_prior = (grp // 2 > 0).astype(jnp.int32)
    high = lax.axis_index("tile") // 2
    place = jnp.stack([early, pair_has_prior, pair, high]).astype(jnp.int32)
    sent = prep(query_states, key_states, value_states, head_weight)
    sent, spatial_weight, noisy_latent = lax.optimization_barrier(
        (sent, spatial_weight, noisy_latent)
    )
    window = window_weights(spatial_weight)
    halo_noisy = with_halo(noisy_latent[0], (("head", 2), ("tile", 1)), 1)
    halo_noisy = halo_noisy.reshape(2, 2, 4, 8, LAT).transpose(1, 2, 3, 0, 4).reshape(64, HD)
    recv = lax.all_to_all(sent, AXES, 0, 0, tiled=True, axis_index_groups=groups)
    late_kv = late_part(place, recv, (halo_noisy, window))
    prior = lax.ppermute(late_kv, AXES, prior_route(groups))
    late, top, mix = attend_here(place, recv)
    partial = attend_prior(place, recv, prior, late, top, mix)
    back = lax.all_to_all(partial, AXES, 0, 0, tiled=True, axis_index_groups=half_groups(groups))
    own, other = sum_heads(back)
    other = lax.ppermute(other, "tile", [(0, 2), (1, 3), (2, 0), (3, 1)])
    velocity = own + other.astype(jnp.float32)
    clean = halo_noisy - noise_level[0] * velocity
    latent = clean.astype(jnp.bfloat16)
    before = shifted(latent, "grp", 1)
    clean_latent = clean.reshape(2, 4, 8, 2, LAT)[:, 1:3, 1:7].transpose(3, 0, 1, 2, 4)
    clean_latent = clean_latent.reshape(noisy_latent.shape)
    where = jnp.stack([has_prior.astype(jnp.int32), lax.axis_index("tile"), lax.axis_index("head")])
    decoded = decode(
        where,
        before,
        latent,
        inlet_weight.reshape(27 * ZC, CH),
        inlet_bias[None],
        temporal_weight.reshape(3 * CH, 2 * CH),
        temporal_bias[None],
        window,
        spatial_bias[None],
    )
    return (clean_latent, decoded[None])


def solution(mesh):
    return jax.shard_map(
        shards,
        mesh=mesh,
        in_specs=(
            P("grp", None, "tile", "head", None),
            P("grp", None, "tile", "head", None),
            P("grp", None, "tile", "head", None),
            P("grp", None, "tile", "head", None),
            P("grp"),
            P(),
            P(),
            P(),
            P(),
            P(),
            P(),
            P(),
        ),
        out_specs=(P("grp", None, "tile", "head", None), P("grp", None, "tile", "head", None)),
        check_vma=False,
    )
```

```python
import math

import jax
import jax.numpy as jnp
from jax import lax
from jax.experimental import pallas as pl
from jax.experimental.pallas import tpu as pltpu
from jax.sharding import PartitionSpec as P

HD = 128
ZC = 16
HEADS = 32
OWN = 48
LAT = 64
ROWS = 2 * OWN + OWN // 2
AXES = ("grp", "head", "tile")
VMEM_BYTES = 32 * 1024 * 1024


def device_id(y, pair, low, x, high, core):
    return ((y * 4 + 2 * pair + low) * 4 + x) * 4 + 2 * high + core


def pair_groups():
    groups = []
    for y in range(4):
        for pair in range(2):
            members = []
            for a in range(2):
                for x in range(4):
                    for b in range(2):
                        for core in range(2):
                            low = a if pair == 0 else 1 - a
                            high = b if pair == 0 or a == 1 else 1 - b
                            members.append(device_id(y, pair, low, x, high, core))
            groups.append(members)
    return groups


def half_groups(groups):
    return [[d for d in group if d // 2 % 2 == high] for group in groups for high in range(2)]


def prior_route(groups):
    return [(groups[g][k], groups[g + 1][k]) for g in range(len(groups) - 1) for k in range(HEADS)]


PREP_STEPS = 2
PREP_HEADS = HEADS // PREP_STEPS


def prep_kernel(query_ref, key_ref, value_ref, weight_ref, out_ref):
    dims = (((1,), (1,)), ((), ()))
    width = PREP_HEADS * HD
    query = query_ref[0].reshape(OWN, width)
    key = key_ref[0].reshape(OWN, width)
    value = value_ref[0].reshape(OWN, width)
    for h in range(PREP_HEADS):
        lanes = slice(h * HD, (h + 1) * HD)
        out_ref[h, 0:OWN, :] = query[:, lanes]
        out_ref[h, OWN : 2 * OWN, :] = key[:, lanes]
        folded = lax.dot_general(
            value[:, lanes], weight_ref[:, lanes], dims, preferred_element_type=jnp.float32
        )
        packed = jnp.concatenate([folded[: OWN // 2], folded[OWN // 2 :]], axis=1)
        out_ref[h, 2 * OWN : ROWS, :] = packed.astype(jnp.bfloat16)


def own_order(states):
    return pltpu.with_memory_space_constraint(states.transpose(0, 1, 3, 2, 4), pltpu.HBM)


def prep(query, key, value, weight):
    width = PREP_HEADS * HD
    tile = pl.BlockSpec((1, 4, 6, 2, width), lambda i: (0, 0, 0, 0, i))
    return pl.pallas_call(
        prep_kernel,
        grid=(PREP_STEPS,),
        out_shape=jax.ShapeDtypeStruct((HEADS, ROWS, HD), jnp.bfloat16),
        in_specs=[tile, tile, tile, pl.BlockSpec((LAT, width), lambda i: (0, i))],
        out_specs=pl.BlockSpec((PREP_HEADS, ROWS, HD), lambda i: (i, 0, 0)),
        compiler_params=pltpu.CompilerParams(vmem_limit_bytes=16 * 1024 * 1024),
    )(own_order(query), own_order(key), own_order(value), pltpu.with_memory_space_constraint(weight.T, pltpu.HBM))


def spread_values(packed, target):
    lower = packed[:, :, :LAT].astype(jnp.float32)
    upper = packed[:, :, LAT:].astype(jnp.float32)
    both = jnp.concatenate([lower, upper], axis=1).reshape(16 * OWN, LAT)
    ones = jnp.ones((16 * OWN, HD - LAT), jnp.float32)
    target[...] = jnp.concatenate([both, ones], axis=1).astype(jnp.bfloat16)


def fold_scale():
    return (1.0 / math.sqrt(HD)) * math.log2(math.e)


def scores_of(query, keys):
    dims = (((1,), (1,)), ((), ()))
    return lax.dot_general(query, keys, dims, preferred_element_type=jnp.float32)


def pack_result(mixed, out_ref, start, blocks):
    velocity = mixed[:, :LAT] / mixed[:, LAT : 2 * LAT]
    velocity = velocity.reshape(blocks, OWN, LAT)
    packed = jnp.concatenate([velocity[:, : OWN // 2], velocity[:, OWN // 2 :]], axis=2)
    out_ref[pl.ds(start, blocks)] = packed.astype(out_ref.dtype)


QB = 16
PB = 8


def late_part_kernel(place_ref, recv_ref, *rest):
    rest[-1][...] = recv_ref[pl.ds(16 - place_ref[0], 16), OWN:, :]


def late_part(place, recv, ready):
    vmem = pl.BlockSpec(memory_space=pltpu.VMEM)
    return pl.pallas_call(
        late_part_kernel,
        out_shape=jax.ShapeDtypeStruct((16, ROWS - OWN, HD), jnp.bfloat16),
        in_specs=[pl.BlockSpec(memory_space=pltpu.SMEM), vmem]
        + [pl.BlockSpec(memory_space=pl.ANY)] * len(ready),
        out_specs=vmem,
        compiler_params=pltpu.CompilerParams(vmem_limit_bytes=4 * 1024 * 1024),
    )(place, recv, *ready)


def attend_here_kernel(
    place_ref, recv_ref, out_hbm, max_ref, mix_ref, early_v, late_v, packed_ref, grid_ref, out_ref, sem
):
    early = place_ref[0]
    late = 16 - early
    spread_values(recv_ref[pl.ds(early, 16), 2 * OWN :, :], early_v)
    spread_values(recv_ref[pl.ds(late, 16), 2 * OWN :, :], late_v)
    early_k = recv_ref[pl.ds(early, 16), OWN : 2 * OWN, :].reshape(16 * OWN, HD)
    late_k = recv_ref[pl.ds(late, 16), OWN : 2 * OWN, :].reshape(16 * OWN, HD)
    scale = fold_scale()

    def late_block(i, carry):
        query = recv_ref[pl.ds(late + i * QB, QB), :OWN, :].reshape(QB * OWN, HD)
        here = scores_of(query, late_k) * scale
        before = scores_of(query, early_k) * scale
        top = jnp.maximum(
            jnp.max(here, axis=1, keepdims=True), jnp.max(before, axis=1, keepdims=True)
        )
        here = jnp.exp2(here - top).astype(jnp.bfloat16)
        before = jnp.exp2(before - top).astype(jnp.bfloat16)
        mixed = jnp.dot(here, late_v[...], preferred_element_type=jnp.float32)
        mixed += jnp.dot(before, early_v[...], preferred_element_type=jnp.float32)
        pack_result(mixed, packed_ref, i * QB, QB)
        return carry

    lax.fori_loop(0, 16 // QB, late_block, 0)
    pair = place_ref[2]
    scatter_halo(packed_ref, grid_ref, out_ref, place_ref[3], pair)
    copy = pltpu.make_async_copy(out_ref, out_hbm.at[pl.ds(8 - 8 * pair, 8)], sem)
    copy.start()

    def early_block(i, carry):
        query = recv_ref[pl.ds(early + i * QB, QB), :OWN, :].reshape(QB * OWN, HD)
        here = scores_of(query, early_k) * scale
        top = jnp.max(here, axis=1, keepdims=True)
        here = jnp.exp2(here - top).astype(jnp.bfloat16)
        mix_ref[pl.ds(i * QB * OWN, QB * OWN), :] = jnp.dot(
            here, early_v[...], preferred_element_type=jnp.float32
        )
        max_ref[pl.ds(i * QB * OWN, QB * OWN), :] = jnp.broadcast_to(top, (QB * OWN, HD))
        return carry

    lax.fori_loop(0, 16 // QB, early_block, 0)
    copy.wait()


def halo_scratch():
    return [
        pltpu.VMEM((16, OWN // 2, HD), jnp.float32),
        pltpu.VMEM((4, 2, 10, 8, HD), jnp.float32),
        pltpu.VMEM((8, 128, HD), jnp.bfloat16),
        pltpu.SemaphoreType.DMA,
    ]


def attend_here(place, recv):
    vmem = pl.BlockSpec(memory_space=pltpu.VMEM)
    tokens = 16 * OWN
    return pl.pallas_call(
        attend_here_kernel,
        out_shape=(
            pltpu.HBM((16, 128, HD), jnp.bfloat16),
            jax.ShapeDtypeStruct((tokens, HD), jnp.float32),
            jax.ShapeDtypeStruct((tokens, HD), jnp.float32),
        ),
        in_specs=[pl.BlockSpec(memory_space=pltpu.SMEM), vmem],
        out_specs=(pl.BlockSpec(memory_space=pltpu.HBM), vmem, vmem),
        scratch_shapes=[pltpu.VMEM((tokens, HD), jnp.bfloat16)] * 2 + halo_scratch(),
        compiler_params=pltpu.CompilerParams(vmem_limit_bytes=VMEM_BYTES),
        cost_estimate=pl.CostEstimate(
            flops=4 * 3 * tokens * tokens * HD, bytes_accessed=4 << 20, transcendentals=3 * tokens * tokens
        ),
    )(place, recv)


def attend_prior_kernel(
    place_ref, recv_ref, prior_ref, max_ref, mix_ref, late_hbm, out_hbm, prior_v, packed_ref, grid_ref,
    out_ref, sem,
):
    early = place_ref[0]
    penalty = jnp.where(place_ref[1] > 0, 0.0, -1e30).astype(jnp.float32)
    spread_values(prior_ref[:, OWN:, :], prior_v)
    prior_k = prior_ref[:, :OWN, :].reshape(16 * OWN, HD)
    scale = fold_scale()

    def block(i, carry):
        rows = pl.ds(i * PB * OWN, PB * OWN)
        query = recv_ref[pl.ds(early + i * PB, PB), :OWN, :].reshape(PB * OWN, HD)
        before = scores_of(query, prior_k) * scale + penalty
        old = max_ref[rows, :]
        top = jnp.maximum(old[:, :1], jnp.max(before, axis=1, keepdims=True))
        before = jnp.exp2(before - top).astype(jnp.bfloat16)
        mixed = jnp.dot(before, prior_v[...], preferred_element_type=jnp.float32)
        mixed += mix_ref[rows, :] * jnp.exp2(old - top)
        pack_result(mixed, packed_ref, i * PB, PB)
        return carry

    lax.fori_loop(0, 16 // PB, block, 0, unroll=True)
    scatter_halo(packed_ref, grid_ref, out_ref, place_ref[3], 0)
    copy = pltpu.make_async_copy(out_ref, out_hbm.at[pl.ds(8 * place_ref[2], 8)], sem)
    copy.start()
    copy.wait()


def scatter_halo(packed_ref, grid_ref, out_ref, high, flip):
    grid_ref[...] = jnp.zeros_like(grid_ref)
    for b in range(2):
        tile_high = b + flip * (1 - 2 * b)
        for core in range(2):
            row = 2 * (2 * tile_high + core) + 1
            for x in range(4):
                block = x * 4 + b * 2 + core
                for frame in range(2):
                    for sub in range(2):
                        line = packed_ref[block, pl.ds(frame * 12 + sub, 6, stride=2), :]
                        grid_ref[x, frame, row + sub, 1:7, :] = line
                        if x < 3:
                            grid_ref[x + 1, frame, row + sub, 0:1, :] = line[5:6]
                        if x > 0:
                            grid_ref[x - 1, frame, row + sub, 7:8, :] = line[0:1]
    for x in range(4):
        for core in range(2):
            for part in range(2):
                row = 2 * (2 * (high if part == 0 else 1 - high) + core)
                tile = grid_ref[x, :, pl.ds(row, 4), :, :].reshape(64, HD)
                out_ref[x * 2 + core, part * 64 : (part + 1) * 64, :] = tile.astype(jnp.bfloat16)


def attend_prior(place, recv, prior, top, mix, sent):
    vmem = pl.BlockSpec(memory_space=pltpu.VMEM)
    hbm = pl.BlockSpec(memory_space=pltpu.HBM)
    tokens = 16 * OWN
    return pl.pallas_call(
        attend_prior_kernel,
        out_shape=pltpu.HBM((16, 128, HD), jnp.bfloat16),
        in_specs=[pl.BlockSpec(memory_space=pltpu.SMEM)] + [vmem] * 4 + [hbm],
        out_specs=hbm,
        input_output_aliases={5: 0},
        scratch_shapes=[pltpu.VMEM((tokens, HD), jnp.bfloat16)] + halo_scratch(),
        compiler_params=pltpu.CompilerParams(vmem_limit_bytes=VMEM_BYTES),
    )(place, recv, prior, top, mix, sent)


def sum_kernel(back_ref, own_ref, other_ref):
    total = back_ref[0].astype(jnp.float32)
    for k in range(1, 16):
        total += back_ref[k].astype(jnp.float32)
    own_ref[...] = total[:64]
    other_ref[...] = total[64:].astype(jnp.bfloat16)


def sum_heads(back):
    vmem = pl.BlockSpec(memory_space=pltpu.VMEM)
    return pl.pallas_call(
        sum_kernel,
        out_shape=(
            jax.ShapeDtypeStruct((64, HD), jnp.float32),
            jax.ShapeDtypeStruct((64, HD), jnp.bfloat16),
        ),
        in_specs=[vmem],
        out_specs=(vmem, vmem),
        compiler_params=pltpu.CompilerParams(vmem_limit_bytes=4 * 1024 * 1024),
    )(back)


CH = 384
OC = 192
TAPS = {(0, 0): (0, 1), (0, 1): (2,), (1, 0): (0,), (1, 1): (1, 2)}


def spread_inlet(inlet_ref, wide_ref):
    blank = jnp.zeros((ZC, CH), jnp.bfloat16)
    for frame in range(3):
        for u in range(4):
            for v in range(4):
                row = frame * 256 + (u // 2 * 2 + v // 2) * LAT + (u % 2 * 2 + v % 2) * ZC
                for sub in range(4):
                    b, e = u - sub // 2, v - sub % 2
                    tap = blank
                    if 0 <= b < 3 and 0 <= e < 3:
                        first = ((frame * 3 + b) * 3 + e) * ZC
                        tap = inlet_ref[first : first + ZC, :]
                    wide_ref[row : row + ZC, sub * CH : (sub + 1) * CH] = tap


def window_kernel(spatial_ref, window_ref):
    for wy in range(2):
        for wx in range(2):
            rows = slice((2 * wy + wx) * CH, (2 * wy + wx + 1) * CH)
            rest = []
            for oy in range(2):
                for ox in range(2):
                    total = None
                    for b in TAPS[oy, wy]:
                        for e in TAPS[ox, wx]:
                            tap = spatial_ref[b, e].astype(jnp.float32)
                            total = tap if total is None else total + tap
                    out = 2 * oy + ox
                    window_ref[rows, out * 128 : (out + 1) * 128] = total[:, :128].astype(jnp.bfloat16)
                    rest.append(total[:, 128:])
            for oy in range(2):
                both = jnp.concatenate([rest[2 * oy], rest[2 * oy + 1]], axis=1)
                window_ref[rows, (4 + oy) * 128 : (5 + oy) * 128] = both.astype(jnp.bfloat16)


def window_weights(spatial_weight):
    vmem = pl.BlockSpec(memory_space=pltpu.VMEM)
    return pl.pallas_call(
        window_kernel,
        out_shape=jax.ShapeDtypeStruct((4 * CH, 4 * OC), jnp.bfloat16),
        in_specs=[vmem],
        out_specs=vmem,
        compiler_params=pltpu.CompilerParams(vmem_limit_bytes=16 * 1024 * 1024),
        cost_estimate=pl.CostEstimate(flops=4 << 20, bytes_accessed=4 << 20, transcendentals=0),
    )(spatial_weight)


SPACE_START = (0, 96, 192, 256)
WIN = 24


def decode_kernel(
    place_ref, before_ref, now_ref, inlet_ref, inlet_bias_ref, time_hbm, time_bias_ref, window_hbm,
    space_bias_ref, out_hbm, patch_ref, feature_ref, time_in_ref, double_ref, shift_ref, space_in_ref,
    low_ref, rest_ref, wide_ref, time_ref, window_ref, out_ref, sems,
):
    time_copy = pltpu.make_async_copy(time_hbm, time_ref, sems.at[0])
    time_copy.start()
    window_copy = pltpu.make_async_copy(window_hbm, window_ref, sems.at[1])
    window_copy.start()
    has_prior, tile, head = place_ref[0], place_ref[1], place_ref[2]
    spread_inlet(inlet_ref, wide_ref)
    for half, ref in enumerate((before_ref, now_ref)):
        cells = ref[...].astype(jnp.float32)
        after = jnp.concatenate([cells[1:], cells[:1]], axis=0)
        for part in range(2):
            lanes = slice(part * LAT, (part + 1) * LAT)
            pairs = jnp.concatenate([cells[:, lanes], after[:, lanes]], axis=1)
            for frame in range(2):
                row = (half * 4 + part * 2 + frame) * WIN
                patch_ref[row : row + WIN, :128] = pairs[frame * 32 : frame * 32 + WIN]
                patch_ref[row : row + WIN, 128:] = pairs[frame * 32 + 8 : frame * 32 + 8 + WIN]
    taps = [patch_ref[a * WIN : (a + 6) * WIN, :].astype(jnp.bfloat16) for a in range(3)]
    features = jnp.dot(
        jnp.concatenate(taps, axis=1), wide_ref[...], preferred_element_type=jnp.float32
    )
    frame_row = lax.broadcasted_iota(jnp.int32, (6 * WIN, 1), 0)
    keep = jnp.logical_or(frame_row >= 2 * WIN, has_prior > 0)
    for sub in range(4):
        lanes = slice(sub * CH, (sub + 1) * CH)
        value = jnp.where(keep, features[:, lanes] + inlet_bias_ref[...], 0.0)
        feature_ref[:, lanes] = value
    for sub in range(4):
        for a in range(3):
            time_in_ref[sub * 96 : (sub + 1) * 96, a * CH : (a + 1) * CH] = feature_ref[
                a * WIN : a * WIN + 96, sub * CH : (sub + 1) * CH
            ].astype(jnp.bfloat16)
    time_copy.wait()
    doubled = jnp.dot(time_in_ref[...], time_ref[...], preferred_element_type=jnp.float32)
    place = lax.broadcasted_iota(jnp.int32, (96, 1), 0)
    window_row = lax.rem(place, WIN) // 8
    window_col = lax.rem(place, 8)
    for sub in range(4):
        row = 4 * tile + 2 * window_row - 1 + sub // 2
        col = 12 * head + 2 * window_col - 1 + sub % 2
        inside = jnp.logical_and(
            jnp.logical_and(row >= 0, row < 16), jnp.logical_and(col >= 0, col < 48)
        )
        value = jnp.where(inside, doubled[sub * 96 : (sub + 1) * 96] + time_bias_ref[...], 0.0)
        double_ref[sub, :96, :] = value
        double_ref[sub, 96:, :] = jnp.zeros((16, 2 * CH), jnp.float32)
        if sub % 2 == 0:
            shift_ref[sub // 2, :103, :] = double_ref[sub, 1:104, :]
            shift_ref[sub // 2, 103:, :] = jnp.zeros((9, 2 * CH), jnp.float32)
    low_bias = space_bias_ref[:, :128]
    rest_bias = space_bias_ref[:, 128:]
    copies = []
    for half in range(2):
        for py in range(2):
            for px in range(2):
                start = SPACE_START[2 * py + px]
                for wy in range(2):
                    for wx in range(2):
                        alpha, beta = (py + wy) % 2, (px + wx) % 2
                        ref = shift_ref.at[alpha] if px + wx == 2 else double_ref.at[2 * alpha + beta]
                        piece = slice((2 * wy + wx) * CH, (2 * wy + wx + 1) * CH)
                        for u in range(2):
                            lanes = slice(u * CH, (u + 1) * CH)
                            if py == 0:
                                spans = [(half * 2 * WIN, start + u * 2 * WIN, 2 * WIN)]
                            else:
                                spans = [
                                    ((half * 2 + t) * WIN + wy * 8, start + (u * 2 + t) * 16, 16)
                                    for t in range(2)
                                ]
                            for source, target, rows in spans:
                                space_in_ref[half, target : target + rows, piece] = ref[
                                    source : source + rows, lanes
                                ].astype(jnp.bfloat16)
        if half == 0:
            window_copy.wait()
        mixed = jnp.dot(space_in_ref[half], window_ref[...], preferred_element_type=jnp.float32)
        for py in range(2):
            for px in range(2):
                for oy in range(2):
                    for ox in range(2):
                        column = 8 - 1 + 2 * px + ox
                        out = 2 * oy + ox
                        for ri in range(3 - py):
                            high = 4 * ri - 1 + 2 * py + oy
                            if not 0 <= high < 8:
                                continue
                            for u in range(2):
                                for t in range(2):
                                    row = SPACE_START[2 * py + px] + ri * 8
                                    row += (u * 2 + t) * (WIN if py == 0 else 16)
                                    low = mixed[row : row + 8, out * 128 : (out + 1) * 128]
                                    rest = mixed[row : row + 8, (4 + oy) * 128 : (5 + oy) * 128]
                                    if ox:
                                        rest = pltpu.roll(rest, 64, 1)
                                    spot = pl.ds(column, 8, stride=4)
                                    line = (2 * (half * 2 + t) + u) * 8 + high
                                    low_ref[line, spot, :] = low
                                    rest_ref[line, spot, :] = rest
        for frame in range(half * 4, half * 4 + 4):
            for high in range(8):
                line = frame * 8 + high
                out_ref[frame, high, :, :128] = (low_ref[line, 8:32, :] + low_bias).astype(
                    jnp.bfloat16
                )
                out_ref[frame, high, :, 128:] = (rest_ref[line, 8:32, :LAT] + rest_bias).astype(
                    jnp.bfloat16
                )
        frames = pl.ds(half * 4, 4)
        copy = pltpu.make_async_copy(out_ref.at[frames], out_hbm.at[frames], sems.at[2 + half])
        copy.start()
        copies.append(copy)
    for copy in copies:
        copy.wait()


def decode(place, before, now, inlet, inlet_bias, time_weight, time_bias, window, space_bias):
    vmem = pl.BlockSpec(memory_space=pltpu.VMEM)
    hbm = pl.BlockSpec(memory_space=pltpu.HBM)
    f32, bf16 = jnp.float32, jnp.bfloat16
    time_weight = pltpu.with_memory_space_constraint(time_weight, pltpu.HBM)
    window = pltpu.with_memory_space_constraint(window, pltpu.HBM)
    return pl.pallas_call(
        decode_kernel,
        out_shape=pltpu.HBM((8, 8, 24, OC), bf16),
        in_specs=[pl.BlockSpec(memory_space=pltpu.SMEM)] + [vmem] * 4 + [hbm, vmem, hbm, vmem],
        out_specs=hbm,
        scratch_shapes=[
            pltpu.VMEM((8 * WIN, 256), f32),
            pltpu.VMEM((6 * WIN, 4 * CH), f32),
            pltpu.VMEM((384, 3 * CH), bf16),
            pltpu.VMEM((4, 112, 2 * CH), f32),
            pltpu.VMEM((2, 112, 2 * CH), f32),
            pltpu.VMEM((2, 320, 4 * CH), bf16),
            pltpu.VMEM((64, 40, 128), f32),
            pltpu.VMEM((64, 40, 128), f32),
            pltpu.VMEM((768, 4 * CH), bf16),
            pltpu.VMEM((3 * CH, 2 * CH), bf16),
            pltpu.VMEM((4 * CH, 4 * OC), bf16),
            pltpu.VMEM((8, 8, 24, OC), bf16),
            pltpu.SemaphoreType.DMA((4,)),
        ],
        compiler_params=pltpu.CompilerParams(vmem_limit_bytes=VMEM_BYTES),
    )(place, before, now, inlet, inlet_bias, time_weight, time_bias, window, space_bias)


def shifted(block, axis, distance):
    devices = range(lax.axis_size(axis))
    route = [(i - distance, i) for i in devices if i - distance in devices]
    return lax.ppermute(block, axis, route)


def with_halo(cells, sides, width):
    for axis, dim in sides:
        count = lax.axis_size(axis)
        ends = count - 1
        head = lax.slice_in_dim(cells, 0, width, axis=dim)
        tail = lax.slice_in_dim(cells, cells.shape[dim] - width, cells.shape[dim], axis=dim)
        cells = jnp.concatenate(
            [
                lax.ppermute(tail, axis, [(i, (i + 1) % count) for i in range(ends)]),
                cells,
                lax.ppermute(head, axis, [((i + 1) % count, i) for i in range(ends)]),
            ],
            axis=dim,
        )
    return cells


def shards(
    query_states,
    key_states,
    value_states,
    noisy_latent,
    noise_level,
    head_weight,
    inlet_weight,
    inlet_bias,
    temporal_weight,
    temporal_bias,
    spatial_weight,
    spatial_bias,
):
    groups = pair_groups()
    grp = lax.axis_index("grp")
    pair = (grp // 2) % 2
    has_prior = grp > 0
    early = 16 * pair
    pair_has_prior = (grp // 2 > 0).astype(jnp.int32)
    high = lax.axis_index("tile") // 2
    place = jnp.stack([early, pair_has_prior, pair, high]).astype(jnp.int32)
    sent = prep(query_states, key_states, value_states, head_weight)
    sent, spatial_weight, noisy_latent = lax.optimization_barrier(
        (sent, spatial_weight, noisy_latent)
    )
    window = window_weights(spatial_weight)
    halo_noisy = with_halo(noisy_latent[0], (("head", 2), ("tile", 1)), 1)
    halo_noisy = halo_noisy.reshape(2, 2, 4, 8, LAT).transpose(1, 2, 3, 0, 4).reshape(64, HD)
    recv = lax.all_to_all(sent, AXES, 0, 0, tiled=True, axis_index_groups=groups)
    late_kv = late_part(place, recv, (halo_noisy, window))
    prior = lax.ppermute(late_kv, AXES, prior_route(groups))
    partial, top, mix = attend_here(place, recv)
    partial = attend_prior(place, recv, prior, top, mix, partial)
    back = lax.all_to_all(partial, AXES, 0, 0, tiled=True, axis_index_groups=half_groups(groups))
    own, other = sum_heads(back)
    other = lax.ppermute(other, "tile", [(0, 2), (1, 3), (2, 0), (3, 1)])
    velocity = own + other.astype(jnp.float32)
    clean = halo_noisy - noise_level[0] * velocity
    latent = clean.astype(jnp.bfloat16)
    before = shifted(latent, "grp", 1)
    clean_latent = clean.reshape(2, 4, 8, 2, LAT)[:, 1:3, 1:7].transpose(3, 0, 1, 2, 4)
    clean_latent = clean_latent.reshape(noisy_latent.shape)
    where = jnp.stack([has_prior.astype(jnp.int32), lax.axis_index("tile"), lax.axis_index("head")])
    decoded = decode(
        where,
        before,
        latent,
        inlet_weight.reshape(27 * ZC, CH),
        inlet_bias[None],
        temporal_weight.reshape(3 * CH, 2 * CH),
        temporal_bias[None],
        window,
        spatial_bias[None],
    )
    return (clean_latent, decoded[None])


def solution(mesh):
    return jax.shard_map(
        shards,
        mesh=mesh,
        in_specs=(
            P("grp", None, "tile", "head", None),
            P("grp", None, "tile", "head", None),
            P("grp", None, "tile", "head", None),
            P("grp", None, "tile", "head", None),
            P("grp"),
            P(),
            P(),
            P(),
            P(),
            P(),
            P(),
            P(),
        ),
        out_specs=(P("grp", None, "tile", "head", None), P("grp", None, "tile", "head", None)),
        check_vma=False,
    )
```

```python
import math

import jax
import jax.numpy as jnp
from jax import lax
from jax.experimental import pallas as pl
from jax.experimental.pallas import tpu as pltpu
from jax.sharding import PartitionSpec as P

HD = 128
ZC = 16
HEADS = 32
OWN = 48
LAT = 64
ROWS = 2 * OWN + OWN // 2
AXES = ("grp", "head", "tile")
VMEM_BYTES = 32 * 1024 * 1024


def device_id(y, pair, low, x, high, core):
    return ((y * 4 + 2 * pair + low) * 4 + x) * 4 + 2 * high + core


def pair_groups():
    groups = []
    for y in range(4):
        for pair in range(2):
            members = []
            for a in range(2):
                for x in range(4):
                    for b in range(2):
                        for core in range(2):
                            low = a if pair == 0 else 1 - a
                            high = b if pair == 0 or a == 1 else 1 - b
                            members.append(device_id(y, pair, low, x, high, core))
            groups.append(members)
    return groups


def half_groups(groups):
    return [[d for d in group if d // 2 % 2 == high] for group in groups for high in range(2)]


ACROSS = [(0, 2), (1, 3), (2, 0), (3, 1)]


def span_route(turn):
    return [
        ((span * 4 + x) * 4 + tile, ((span + 1) * 4 + x) * 4 + (tile + turn) % 4)
        for span in range(15)
        for x in range(4)
        for tile in range(4)
    ]


def prior_route(groups):
    return [(groups[g][k], groups[g + 1][k]) for g in range(len(groups) - 1) for k in range(HEADS)]


PREP_STEPS = 2
PREP_HEADS = HEADS // PREP_STEPS


def prep_kernel(query_ref, key_ref, value_ref, weight_ref, out_ref):
    dims = (((1,), (1,)), ((), ()))
    width = PREP_HEADS * HD
    query = query_ref[0].reshape(OWN, width)
    key = key_ref[0].reshape(OWN, width)
    value = value_ref[0].reshape(OWN, width)
    for h in range(PREP_HEADS):
        lanes = slice(h * HD, (h + 1) * HD)
        out_ref[h, 0:OWN, :] = query[:, lanes]
        out_ref[h, OWN : 2 * OWN, :] = key[:, lanes]
        folded = lax.dot_general(
            value[:, lanes], weight_ref[:, lanes], dims, preferred_element_type=jnp.float32
        )
        packed = jnp.concatenate([folded[: OWN // 2], folded[OWN // 2 :]], axis=1)
        out_ref[h, 2 * OWN : ROWS, :] = packed.astype(jnp.bfloat16)


def own_order(states):
    return pltpu.with_memory_space_constraint(states.transpose(0, 1, 3, 2, 4), pltpu.HBM)


def prep(query, key, value, weight):
    width = PREP_HEADS * HD
    tile = pl.BlockSpec((1, 4, 6, 2, width), lambda i: (0, 0, 0, 0, i))
    return pl.pallas_call(
        prep_kernel,
        grid=(PREP_STEPS,),
        out_shape=jax.ShapeDtypeStruct((HEADS, ROWS, HD), jnp.bfloat16),
        in_specs=[tile, tile, tile, pl.BlockSpec((LAT, width), lambda i: (0, i))],
        out_specs=pl.BlockSpec((PREP_HEADS, ROWS, HD), lambda i: (i, 0, 0)),
        compiler_params=pltpu.CompilerParams(vmem_limit_bytes=16 * 1024 * 1024),
    )(own_order(query), own_order(key), own_order(value), pltpu.with_memory_space_constraint(weight.T, pltpu.HBM))


def spread_values(packed, target):
    lower = packed[:, :, :LAT].astype(jnp.float32)
    upper = packed[:, :, LAT:].astype(jnp.float32)
    both = jnp.concatenate([lower, upper], axis=1).reshape(16 * OWN, LAT)
    ones = jnp.ones((16 * OWN, HD - LAT), jnp.float32)
    target[...] = jnp.concatenate([both, ones], axis=1).astype(jnp.bfloat16)


def fold_scale():
    return (1.0 / math.sqrt(HD)) * math.log2(math.e)


def scores_of(query, keys):
    dims = (((1,), (1,)), ((), ()))
    return lax.dot_general(query, keys, dims, preferred_element_type=jnp.float32)


def pack_result(mixed, out_ref, start, blocks):
    velocity = mixed[:, :LAT] / mixed[:, LAT : 2 * LAT]
    velocity = velocity.reshape(blocks, OWN, LAT)
    packed = jnp.concatenate([velocity[:, : OWN // 2], velocity[:, OWN // 2 :]], axis=2)
    out_ref[pl.ds(start, blocks)] = packed.astype(out_ref.dtype)


QB = 16
PB = 8


def late_part_kernel(place_ref, recv_ref, *rest):
    rest[-1][...] = recv_ref[pl.ds(16 - place_ref[0], 16), OWN:, :]


def late_part(place, recv, ready):
    vmem = pl.BlockSpec(memory_space=pltpu.VMEM)
    return pl.pallas_call(
        late_part_kernel,
        out_shape=jax.ShapeDtypeStruct((16, ROWS - OWN, HD), jnp.bfloat16),
        in_specs=[pl.BlockSpec(memory_space=pltpu.SMEM), vmem]
        + [pl.BlockSpec(memory_space=pl.ANY)] * len(ready),
        out_specs=vmem,
        compiler_params=pltpu.CompilerParams(vmem_limit_bytes=4 * 1024 * 1024),
    )(place, recv, *ready)


def attend_here_kernel(
    place_ref, recv_ref, out_hbm, max_ref, mix_ref, early_v, late_v, packed_ref, grid_ref, out_ref, sem
):
    early = place_ref[0]
    late = 16 - early
    spread_values(recv_ref[pl.ds(early, 16), 2 * OWN :, :], early_v)
    spread_values(recv_ref[pl.ds(late, 16), 2 * OWN :, :], late_v)
    early_k = recv_ref[pl.ds(early, 16), OWN : 2 * OWN, :].reshape(16 * OWN, HD)
    late_k = recv_ref[pl.ds(late, 16), OWN : 2 * OWN, :].reshape(16 * OWN, HD)
    scale = fold_scale()

    def late_block(i, carry):
        query = recv_ref[pl.ds(late + i * QB, QB), :OWN, :].reshape(QB * OWN, HD)
        here = scores_of(query, late_k) * scale
        before = scores_of(query, early_k) * scale
        top = jnp.maximum(
            jnp.max(here, axis=1, keepdims=True), jnp.max(before, axis=1, keepdims=True)
        )
        here = jnp.exp2(here - top).astype(jnp.bfloat16)
        before = jnp.exp2(before - top).astype(jnp.bfloat16)
        mixed = jnp.dot(here, late_v[...], preferred_element_type=jnp.float32)
        mixed += jnp.dot(before, early_v[...], preferred_element_type=jnp.float32)
        pack_result(mixed, packed_ref, i * QB, QB)
        return carry

    lax.fori_loop(0, 16 // QB, late_block, 0)
    pair = place_ref[2]
    scatter_halo(packed_ref, grid_ref, out_ref, place_ref[3], pair)
    copy = pltpu.make_async_copy(out_ref, out_hbm.at[pl.ds(8 - 8 * pair, 8)], sem)
    copy.start()

    def early_block(i, carry):
        query = recv_ref[pl.ds(early + i * QB, QB), :OWN, :].reshape(QB * OWN, HD)
        here = scores_of(query, early_k) * scale
        top = jnp.max(here, axis=1, keepdims=True)
        here = jnp.exp2(here - top).astype(jnp.bfloat16)
        mix_ref[pl.ds(i * QB * OWN, QB * OWN), :] = jnp.dot(
            here, early_v[...], preferred_element_type=jnp.float32
        )
        max_ref[pl.ds(i * QB * OWN, QB * OWN), :] = jnp.broadcast_to(top, (QB * OWN, HD))
        return carry

    lax.fori_loop(0, 16 // QB, early_block, 0)
    copy.wait()


def halo_scratch():
    return [
        pltpu.VMEM((16, OWN // 2, HD), jnp.float32),
        pltpu.VMEM((4, 2, 10, 8, HD), jnp.float32),
        pltpu.VMEM((8, 128, HD), jnp.bfloat16),
        pltpu.SemaphoreType.DMA,
    ]


def attend_here(place, recv):
    vmem = pl.BlockSpec(memory_space=pltpu.VMEM)
    tokens = 16 * OWN
    return pl.pallas_call(
        attend_here_kernel,
        out_shape=(
            pltpu.HBM((16, 128, HD), jnp.bfloat16),
            jax.ShapeDtypeStruct((tokens, HD), jnp.float32),
            jax.ShapeDtypeStruct((tokens, HD), jnp.float32),
        ),
        in_specs=[pl.BlockSpec(memory_space=pltpu.SMEM), vmem],
        out_specs=(pl.BlockSpec(memory_space=pltpu.HBM), vmem, vmem),
        scratch_shapes=[pltpu.VMEM((tokens, HD), jnp.bfloat16)] * 2 + halo_scratch(),
        compiler_params=pltpu.CompilerParams(vmem_limit_bytes=VMEM_BYTES),
        cost_estimate=pl.CostEstimate(
            flops=4 * 3 * tokens * tokens * HD, bytes_accessed=4 << 20, transcendentals=3 * tokens * tokens
        ),
    )(place, recv)


def attend_prior_kernel(
    place_ref, recv_ref, prior_ref, max_ref, mix_ref, late_hbm, out_hbm, prior_v, packed_ref, grid_ref,
    out_ref, sem,
):
    early = place_ref[0]
    penalty = jnp.where(place_ref[1] > 0, 0.0, -1e30).astype(jnp.float32)
    spread_values(prior_ref[:, OWN:, :], prior_v)
    prior_k = prior_ref[:, :OWN, :].reshape(16 * OWN, HD)
    scale = fold_scale()

    def block(i, carry):
        rows = pl.ds(i * PB * OWN, PB * OWN)
        query = recv_ref[pl.ds(early + i * PB, PB), :OWN, :].reshape(PB * OWN, HD)
        before = scores_of(query, prior_k) * scale + penalty
        old = max_ref[rows, :]
        top = jnp.maximum(old[:, :1], jnp.max(before, axis=1, keepdims=True))
        before = jnp.exp2(before - top).astype(jnp.bfloat16)
        mixed = jnp.dot(before, prior_v[...], preferred_element_type=jnp.float32)
        mixed += mix_ref[rows, :] * jnp.exp2(old - top)
        pack_result(mixed, packed_ref, i * PB, PB)
        return carry

    lax.fori_loop(0, 16 // PB, block, 0, unroll=True)
    scatter_halo(packed_ref, grid_ref, out_ref, place_ref[3], 0)
    copy = pltpu.make_async_copy(out_ref, out_hbm.at[pl.ds(8 * place_ref[2], 8)], sem)
    copy.start()
    copy.wait()


def scatter_halo(packed_ref, grid_ref, out_ref, high, flip):
    grid_ref[...] = jnp.zeros_like(grid_ref)
    for b in range(2):
        tile_high = b + flip * (1 - 2 * b)
        for core in range(2):
            row = 2 * (2 * tile_high + core) + 1
            for x in range(4):
                block = x * 4 + b * 2 + core
                for frame in range(2):
                    for sub in range(2):
                        line = packed_ref[block, pl.ds(frame * 12 + sub, 6, stride=2), :]
                        grid_ref[x, frame, row + sub, 1:7, :] = line
                        if x < 3:
                            grid_ref[x + 1, frame, row + sub, 0:1, :] = line[5:6]
                        if x > 0:
                            grid_ref[x - 1, frame, row + sub, 7:8, :] = line[0:1]
    for x in range(4):
        for core in range(2):
            for part in range(2):
                row = 2 * (2 * (high if part == 0 else 1 - high) + core)
                tile = grid_ref[x, :, pl.ds(row, 4), :, :].reshape(64, HD)
                out_ref[x * 2 + core, part * 64 : (part + 1) * 64, :] = tile.astype(jnp.bfloat16)


def attend_prior(place, recv, prior, top, mix, sent):
    vmem = pl.BlockSpec(memory_space=pltpu.VMEM)
    hbm = pl.BlockSpec(memory_space=pltpu.HBM)
    tokens = 16 * OWN
    return pl.pallas_call(
        attend_prior_kernel,
        out_shape=pltpu.HBM((16, 128, HD), jnp.bfloat16),
        in_specs=[pl.BlockSpec(memory_space=pltpu.SMEM)] + [vmem] * 4 + [hbm],
        out_specs=hbm,
        input_output_aliases={5: 0},
        scratch_shapes=[pltpu.VMEM((tokens, HD), jnp.bfloat16)] + halo_scratch(),
        compiler_params=pltpu.CompilerParams(vmem_limit_bytes=VMEM_BYTES),
    )(place, recv, prior, top, mix, sent)


def sum_kernel(level_ref, back_ref, noisy_ref, own_ref, own_sent_ref, other_ref):
    total = back_ref[0].astype(jnp.float32)
    for k in range(1, 16):
        total += back_ref[k].astype(jnp.float32)
    own = noisy_ref[...] - level_ref[0] * total[:64]
    own_ref[...] = own
    own_sent_ref[...] = own.astype(jnp.bfloat16)
    other_ref[...] = (-level_ref[0] * total[64:]).astype(jnp.bfloat16)


def sum_heads(level, back, noisy):
    vmem = pl.BlockSpec(memory_space=pltpu.VMEM)
    return pl.pallas_call(
        sum_kernel,
        out_shape=(
            jax.ShapeDtypeStruct((64, HD), jnp.float32),
            jax.ShapeDtypeStruct((64, HD), jnp.bfloat16),
            jax.ShapeDtypeStruct((64, HD), jnp.bfloat16),
        ),
        in_specs=[pl.BlockSpec(memory_space=pltpu.SMEM), vmem, vmem],
        out_specs=(vmem, vmem, vmem),
        compiler_params=pltpu.CompilerParams(vmem_limit_bytes=4 * 1024 * 1024),
    )(level, back, noisy)


CH = 384
OC = 192
TAPS = {(0, 0): (0, 1), (0, 1): (2,), (1, 0): (0,), (1, 1): (1, 2)}


def spread_inlet(inlet_ref, wide_ref):
    blank = jnp.zeros((ZC, CH), jnp.bfloat16)
    for frame in range(3):
        for u in range(4):
            for v in range(4):
                row = frame * 256 + (u // 2 * 2 + v // 2) * LAT + (u % 2 * 2 + v % 2) * ZC
                for sub in range(4):
                    b, e = u - sub // 2, v - sub % 2
                    tap = blank
                    if 0 <= b < 3 and 0 <= e < 3:
                        first = ((frame * 3 + b) * 3 + e) * ZC
                        tap = inlet_ref[first : first + ZC, :]
                    wide_ref[row : row + ZC, sub * CH : (sub + 1) * CH] = tap


def ready_kernel(inlet_ref, time_hbm, window_hbm, order_ref, wide_ref, time_ref, window_ref, sems):
    copies = (
        pltpu.make_async_copy(time_hbm, time_ref, sems.at[0]),
        pltpu.make_async_copy(window_hbm, window_ref, sems.at[1]),
    )
    for copy in copies:
        copy.start()
    spread_inlet(inlet_ref, wide_ref)
    for copy in copies:
        copy.wait()


def ready_weights(inlet, time_weight, window, order):
    vmem = pl.BlockSpec(memory_space=pltpu.VMEM)
    hbm = pl.BlockSpec(memory_space=pltpu.HBM)
    return pl.pallas_call(
        ready_kernel,
        out_shape=(
            pltpu.VMEM((768, 4 * CH), jnp.bfloat16),
            pltpu.VMEM((3 * CH, 2 * CH), jnp.bfloat16),
            pltpu.VMEM((4 * CH, 4 * OC), jnp.bfloat16),
        ),
        in_specs=[vmem, hbm, hbm, pl.BlockSpec(memory_space=pl.ANY)],
        out_specs=(vmem, vmem, vmem),
        scratch_shapes=[pltpu.SemaphoreType.DMA((2,))],
        compiler_params=pltpu.CompilerParams(vmem_limit_bytes=12 * 1024 * 1024),
        cost_estimate=pl.CostEstimate(flops=4 << 20, bytes_accessed=8 << 20, transcendentals=0),
    )(
        inlet,
        pltpu.with_memory_space_constraint(time_weight, pltpu.HBM),
        pltpu.with_memory_space_constraint(window, pltpu.HBM),
        order,
    )


def window_kernel(spatial_ref, window_ref):
    for wy in range(2):
        for wx in range(2):
            rows = slice((2 * wy + wx) * CH, (2 * wy + wx + 1) * CH)
            rest = []
            for oy in range(2):
                for ox in range(2):
                    total = None
                    for b in TAPS[oy, wy]:
                        for e in TAPS[ox, wx]:
                            tap = spatial_ref[b, e].astype(jnp.float32)
                            total = tap if total is None else total + tap
                    out = 2 * oy + ox
                    window_ref[rows, out * 128 : (out + 1) * 128] = total[:, :128].astype(jnp.bfloat16)
                    rest.append(total[:, 128:])
            for oy in range(2):
                both = jnp.concatenate([rest[2 * oy], rest[2 * oy + 1]], axis=1)
                window_ref[rows, (4 + oy) * 128 : (5 + oy) * 128] = both.astype(jnp.bfloat16)


def window_weights(spatial_weight):
    vmem = pl.BlockSpec(memory_space=pltpu.VMEM)
    return pl.pallas_call(
        window_kernel,
        out_shape=jax.ShapeDtypeStruct((4 * CH, 4 * OC), jnp.bfloat16),
        in_specs=[vmem],
        out_specs=vmem,
        compiler_params=pltpu.CompilerParams(vmem_limit_bytes=16 * 1024 * 1024),
        cost_estimate=pl.CostEstimate(flops=4 << 20, bytes_accessed=4 << 20, transcendentals=0),
    )(spatial_weight)


SPACE_START = (0, 96, 192, 256)
WIN = 24


def decode_kernel(
    place_ref, before_own_ref, before_other_ref, own_ref, other_ref, wide_ref, inlet_bias_ref, time_ref, time_bias_ref, window_ref,
    space_bias_ref, out_hbm, patch_ref, feature_ref, time_in_ref, double_ref, shift_ref, space_in_ref,
    low_ref, rest_ref, out_ref, sems,
):
    has_prior, tile, head = place_ref[0], place_ref[1], place_ref[2]
    for half, (one_ref, two_ref) in enumerate(((before_own_ref, before_other_ref), (own_ref, other_ref))):
        cells = one_ref[...].astype(jnp.float32) + two_ref[...].astype(jnp.float32)
        cells = cells.astype(jnp.bfloat16).astype(jnp.float32)
        after = jnp.concatenate([cells[1:], cells[:1]], axis=0)
        for part in range(2):
            lanes = slice(part * LAT, (part + 1) * LAT)
            pairs = jnp.concatenate([cells[:, lanes], after[:, lanes]], axis=1)
            for frame in range(2):
                row = (half * 4 + part * 2 + frame) * WIN
                patch_ref[row : row + WIN, :128] = pairs[frame * 32 : frame * 32 + WIN]
                patch_ref[row : row + WIN, 128:] = pairs[frame * 32 + 8 : frame * 32 + 8 + WIN]
    taps = [patch_ref[a * WIN : (a + 6) * WIN, :].astype(jnp.bfloat16) for a in range(3)]
    features = jnp.dot(
        jnp.concatenate(taps, axis=1), wide_ref[...], preferred_element_type=jnp.float32
    )
    frame_row = lax.broadcasted_iota(jnp.int32, (6 * WIN, 1), 0)
    keep = jnp.logical_or(frame_row >= 2 * WIN, has_prior > 0)
    for sub in range(4):
        lanes = slice(sub * CH, (sub + 1) * CH)
        value = jnp.where(keep, features[:, lanes] + inlet_bias_ref[...], 0.0)
        feature_ref[:, lanes] = value
    for sub in range(4):
        for a in range(3):
            time_in_ref[sub * 96 : (sub + 1) * 96, a * CH : (a + 1) * CH] = feature_ref[
                a * WIN : a * WIN + 96, sub * CH : (sub + 1) * CH
            ].astype(jnp.bfloat16)
    doubled = jnp.dot(time_in_ref[...], time_ref[...], preferred_element_type=jnp.float32)
    place = lax.broadcasted_iota(jnp.int32, (96, 1), 0)
    window_row = lax.rem(place, WIN) // 8
    window_col = lax.rem(place, 8)
    for sub in range(4):
        row = 4 * tile + 2 * window_row - 1 + sub // 2
        col = 12 * head + 2 * window_col - 1 + sub % 2
        inside = jnp.logical_and(
            jnp.logical_and(row >= 0, row < 16), jnp.logical_and(col >= 0, col < 48)
        )
        value = jnp.where(inside, doubled[sub * 96 : (sub + 1) * 96] + time_bias_ref[...], 0.0)
        double_ref[sub, :96, :] = value
        double_ref[sub, 96:, :] = jnp.zeros((16, 2 * CH), jnp.float32)
        if sub % 2 == 0:
            shift_ref[sub // 2, :103, :] = double_ref[sub, 1:104, :]
            shift_ref[sub // 2, 103:, :] = jnp.zeros((9, 2 * CH), jnp.float32)
    low_bias = space_bias_ref[:, :128]
    rest_bias = space_bias_ref[:, 128:]
    copies = []
    for half in range(2):
        for py in range(2):
            for px in range(2):
                start = SPACE_START[2 * py + px]
                for wy in range(2):
                    for wx in range(2):
                        alpha, beta = (py + wy) % 2, (px + wx) % 2
                        ref = shift_ref.at[alpha] if px + wx == 2 else double_ref.at[2 * alpha + beta]
                        piece = slice((2 * wy + wx) * CH, (2 * wy + wx + 1) * CH)
                        for u in range(2):
                            lanes = slice(u * CH, (u + 1) * CH)
                            if py == 0:
                                spans = [(half * 2 * WIN, start + u * 2 * WIN, 2 * WIN)]
                            else:
                                spans = [
                                    ((half * 2 + t) * WIN + wy * 8, start + (u * 2 + t) * 16, 16)
                                    for t in range(2)
                                ]
                            for source, target, rows in spans:
                                space_in_ref[half, target : target + rows, piece] = ref[
                                    source : source + rows, lanes
                                ].astype(jnp.bfloat16)
        mixed = jnp.dot(space_in_ref[half], window_ref[...], preferred_element_type=jnp.float32)
        for py in range(2):
            for px in range(2):
                for oy in range(2):
                    for ox in range(2):
                        column = 8 - 1 + 2 * px + ox
                        out = 2 * oy + ox
                        for ri in range(3 - py):
                            high = 4 * ri - 1 + 2 * py + oy
                            if not 0 <= high < 8:
                                continue
                            for u in range(2):
                                for t in range(2):
                                    row = SPACE_START[2 * py + px] + ri * 8
                                    row += (u * 2 + t) * (WIN if py == 0 else 16)
                                    low = mixed[row : row + 8, out * 128 : (out + 1) * 128]
                                    rest = mixed[row : row + 8, (4 + oy) * 128 : (5 + oy) * 128]
                                    if ox:
                                        rest = pltpu.roll(rest, 64, 1)
                                    spot = pl.ds(column, 8, stride=4)
                                    line = (2 * (half * 2 + t) + u) * 8 + high
                                    low_ref[line, spot, :] = low
                                    rest_ref[line, spot, :] = rest
        for frame in range(half * 4, half * 4 + 4):
            for high in range(8):
                line = frame * 8 + high
                out_ref[frame, high, :, :128] = (low_ref[line, 8:32, :] + low_bias).astype(
                    jnp.bfloat16
                )
                out_ref[frame, high, :, 128:] = (rest_ref[line, 8:32, :LAT] + rest_bias).astype(
                    jnp.bfloat16
                )
        frames = pl.ds(half * 4, 4)
        copy = pltpu.make_async_copy(out_ref.at[frames], out_hbm.at[frames], sems.at[half])
        copy.start()
        copies.append(copy)
    for copy in copies:
        copy.wait()


def decode(place, before_own, before_other, own, other, wide, inlet_bias, time_weight, time_bias, window, space_bias):
    vmem = pl.BlockSpec(memory_space=pltpu.VMEM)
    hbm = pl.BlockSpec(memory_space=pltpu.HBM)
    f32, bf16 = jnp.float32, jnp.bfloat16
    wide, time_weight, window = (
        pltpu.with_memory_space_constraint(weight, pltpu.VMEM) for weight in (wide, time_weight, window)
    )
    return pl.pallas_call(
        decode_kernel,
        out_shape=pltpu.HBM((8, 8, 24, OC), bf16),
        in_specs=[pl.BlockSpec(memory_space=pltpu.SMEM)] + [vmem] * 10,
        out_specs=hbm,
        scratch_shapes=[
            pltpu.VMEM((8 * WIN, 256), f32),
            pltpu.VMEM((6 * WIN, 4 * CH), f32),
            pltpu.VMEM((384, 3 * CH), bf16),
            pltpu.VMEM((4, 112, 2 * CH), f32),
            pltpu.VMEM((2, 112, 2 * CH), f32),
            pltpu.VMEM((2, 320, 4 * CH), bf16),
            pltpu.VMEM((64, 40, 128), f32),
            pltpu.VMEM((64, 40, 128), f32),
            pltpu.VMEM((8, 8, 24, OC), bf16),
            pltpu.SemaphoreType.DMA((2,)),
        ],
        compiler_params=pltpu.CompilerParams(vmem_limit_bytes=VMEM_BYTES),
    )(place, before_own, before_other, own, other, wide, inlet_bias, time_weight, time_bias, window, space_bias)


def with_halo(cells, sides, width):
    for axis, dim in sides:
        count = lax.axis_size(axis)
        ends = count - 1
        head = lax.slice_in_dim(cells, 0, width, axis=dim)
        tail = lax.slice_in_dim(cells, cells.shape[dim] - width, cells.shape[dim], axis=dim)
        cells = jnp.concatenate(
            [
                lax.ppermute(tail, axis, [(i, (i + 1) % count) for i in range(ends)]),
                cells,
                lax.ppermute(head, axis, [((i + 1) % count, i) for i in range(ends)]),
            ],
            axis=dim,
        )
    return cells


def shards(
    query_states,
    key_states,
    value_states,
    noisy_latent,
    noise_level,
    head_weight,
    inlet_weight,
    inlet_bias,
    temporal_weight,
    temporal_bias,
    spatial_weight,
    spatial_bias,
):
    groups = pair_groups()
    grp = lax.axis_index("grp")
    pair = (grp // 2) % 2
    has_prior = grp > 0
    early = 16 * pair
    pair_has_prior = (grp // 2 > 0).astype(jnp.int32)
    high = lax.axis_index("tile") // 2
    place = jnp.stack([early, pair_has_prior, pair, high]).astype(jnp.int32)
    sent = prep(query_states, key_states, value_states, head_weight)
    sent, spatial_weight, noisy_latent = lax.optimization_barrier(
        (sent, spatial_weight, noisy_latent)
    )
    window = window_weights(spatial_weight)
    halo_noisy = with_halo(noisy_latent[0], (("head", 2), ("tile", 1)), 1)
    halo_noisy = halo_noisy.reshape(2, 2, 4, 8, LAT).transpose(1, 2, 3, 0, 4).reshape(64, HD)
    recv = lax.all_to_all(sent, AXES, 0, 0, tiled=True, axis_index_groups=groups)
    late_kv = late_part(place, recv, (halo_noisy, window))
    prior = lax.ppermute(late_kv, AXES, prior_route(groups))
    partial, top, mix = attend_here(place, recv)
    partial = attend_prior(place, recv, prior, top, mix, partial)
    back = lax.all_to_all(partial, AXES, 0, 0, tiled=True, axis_index_groups=half_groups(groups))
    own, own_sent, other_sent = sum_heads(noise_level, back, halo_noisy)
    across = lax.ppermute(other_sent, "tile", ACROSS)
    before_other = lax.ppermute(other_sent, AXES, span_route(2))
    before_own = lax.ppermute(own_sent, AXES, span_route(0))
    clean = own + across.astype(jnp.float32)
    clean_latent = clean.reshape(2, 4, 8, 2, LAT)[:, 1:3, 1:7].transpose(3, 0, 1, 2, 4)
    clean_latent = clean_latent.reshape(noisy_latent.shape)
    wide, time_ready, window = ready_weights(
        inlet_weight.reshape(27 * ZC, CH), temporal_weight.reshape(3 * CH, 2 * CH), window, clean_latent
    )
    where = jnp.stack([has_prior.astype(jnp.int32), lax.axis_index("tile"), lax.axis_index("head")])
    decoded = decode(
        where,
        before_own,
        before_other,
        own,
        across,
        wide,
        inlet_bias[None],
        time_ready,
        temporal_bias[None],
        window,
        spatial_bias[None],
    )
    return (clean_latent, decoded[None])


def solution(mesh):
    return jax.shard_map(
        shards,
        mesh=mesh,
        in_specs=(
            P("grp", None, "tile", "head", None),
            P("grp", None, "tile", "head", None),
            P("grp", None, "tile", "head", None),
            P("grp", None, "tile", "head", None),
            P("grp"),
            P(),
            P(),
            P(),
            P(),
            P(),
            P(),
            P(),
        ),
        out_specs=(P("grp", None, "tile", "head", None), P("grp", None, "tile", "head", None)),
        check_vma=False,
    )
```

```python
import math

import jax
import jax.numpy as jnp
from jax import lax
from jax.experimental import pallas as pl
from jax.experimental.pallas import tpu as pltpu
from jax.sharding import PartitionSpec as P

HD = 128
ZC = 16
HEADS = 32
OWN = 48
LAT = 64
ROWS = 2 * OWN + OWN // 2
AXES = ("grp", "head", "tile")
VMEM_BYTES = 32 * 1024 * 1024


def device_id(y, pair, low, x, high, core):
    return ((y * 4 + 2 * pair + low) * 4 + x) * 4 + 2 * high + core


def pair_groups():
    groups = []
    for y in range(4):
        for pair in range(2):
            members = []
            for a in range(2):
                for x in range(4):
                    for b in range(2):
                        for core in range(2):
                            low = a if pair == 0 else 1 - a
                            high = b if pair == 0 or a == 1 else 1 - b
                            members.append(device_id(y, pair, low, x, high, core))
            groups.append(members)
    return groups


def half_groups(groups):
    return [[d for d in group if d // 2 % 2 == high] for group in groups for high in range(2)]


ACROSS = [(0, 2), (1, 3), (2, 0), (3, 1)]


def span_route(turn):
    return [
        ((span * 4 + x) * 4 + tile, ((span + 1) * 4 + x) * 4 + (tile + turn) % 4)
        for span in range(15)
        for x in range(4)
        for tile in range(4)
    ]


def prior_route(groups):
    return [(groups[g][k], groups[g + 1][k]) for g in range(len(groups) - 1) for k in range(HEADS)]


PREP_STEPS = 2
PREP_HEADS = HEADS // PREP_STEPS


def prep_kernel(query_ref, key_ref, value_ref, weight_ref, out_ref):
    dims = (((1,), (1,)), ((), ()))
    width = PREP_HEADS * HD
    query = query_ref[0].reshape(OWN, width)
    key = key_ref[0].reshape(OWN, width)
    value = value_ref[0].reshape(OWN, width)
    for h in range(PREP_HEADS):
        lanes = slice(h * HD, (h + 1) * HD)
        out_ref[h, 0:OWN, :] = query[:, lanes]
        out_ref[h, OWN : 2 * OWN, :] = key[:, lanes]
        folded = lax.dot_general(
            value[:, lanes], weight_ref[:, lanes], dims, preferred_element_type=jnp.float32
        )
        packed = jnp.concatenate([folded[: OWN // 2], folded[OWN // 2 :]], axis=1)
        out_ref[h, 2 * OWN : ROWS, :] = packed.astype(jnp.bfloat16)


def own_order(states):
    return pltpu.with_memory_space_constraint(states.transpose(0, 1, 3, 2, 4), pltpu.HBM)


def prep(query, key, value, weight):
    width = PREP_HEADS * HD
    tile = pl.BlockSpec((1, 4, 6, 2, width), lambda i: (0, 0, 0, 0, i))
    return pl.pallas_call(
        prep_kernel,
        grid=(PREP_STEPS,),
        out_shape=jax.ShapeDtypeStruct((HEADS, ROWS, HD), jnp.bfloat16),
        in_specs=[tile, tile, tile, pl.BlockSpec((LAT, width), lambda i: (0, i))],
        out_specs=pl.BlockSpec((PREP_HEADS, ROWS, HD), lambda i: (i, 0, 0)),
        compiler_params=pltpu.CompilerParams(vmem_limit_bytes=16 * 1024 * 1024),
    )(own_order(query), own_order(key), own_order(value), pltpu.with_memory_space_constraint(weight.T, pltpu.HBM))


def spread_values(packed, target):
    lower = packed[:, :, :LAT].astype(jnp.float32)
    upper = packed[:, :, LAT:].astype(jnp.float32)
    both = jnp.concatenate([lower, upper], axis=1).reshape(16 * OWN, LAT)
    ones = jnp.ones((16 * OWN, HD - LAT), jnp.float32)
    target[...] = jnp.concatenate([both, ones], axis=1).astype(jnp.bfloat16)


def fold_scale():
    return (1.0 / math.sqrt(HD)) * math.log2(math.e)


def scores_of(query, keys):
    dims = (((1,), (1,)), ((), ()))
    return lax.dot_general(query, keys, dims, preferred_element_type=jnp.float32)


def pack_result(mixed, out_ref, start, blocks):
    velocity = mixed[:, :LAT] / mixed[:, LAT : 2 * LAT]
    velocity = velocity.reshape(blocks, OWN, LAT)
    packed = jnp.concatenate([velocity[:, : OWN // 2], velocity[:, OWN // 2 :]], axis=2)
    out_ref[pl.ds(start, blocks)] = packed.astype(out_ref.dtype)


QB = 16
PB = 8


def late_part_kernel(place_ref, recv_ref, *rest):
    rest[-1][...] = recv_ref[pl.ds(16 - place_ref[0], 16), OWN:, :]


def late_part(place, recv, ready):
    vmem = pl.BlockSpec(memory_space=pltpu.VMEM)
    return pl.pallas_call(
        late_part_kernel,
        out_shape=jax.ShapeDtypeStruct((16, ROWS - OWN, HD), jnp.bfloat16),
        in_specs=[pl.BlockSpec(memory_space=pltpu.SMEM), vmem]
        + [pl.BlockSpec(memory_space=pl.ANY)] * len(ready),
        out_specs=vmem,
        compiler_params=pltpu.CompilerParams(vmem_limit_bytes=4 * 1024 * 1024),
    )(place, recv, *ready)


def attend_here_kernel(
    place_ref, recv_ref, out_hbm, max_ref, mix_ref, early_v, late_v, packed_ref, grid_ref, out_ref, sem
):
    early = place_ref[0]
    late = 16 - early
    spread_values(recv_ref[pl.ds(early, 16), 2 * OWN :, :], early_v)
    spread_values(recv_ref[pl.ds(late, 16), 2 * OWN :, :], late_v)
    early_k = recv_ref[pl.ds(early, 16), OWN : 2 * OWN, :].reshape(16 * OWN, HD)
    late_k = recv_ref[pl.ds(late, 16), OWN : 2 * OWN, :].reshape(16 * OWN, HD)
    scale = fold_scale()

    def late_block(i, carry):
        query = recv_ref[pl.ds(late + i * QB, QB), :OWN, :].reshape(QB * OWN, HD)
        here = scores_of(query, late_k) * scale
        before = scores_of(query, early_k) * scale
        top = jnp.maximum(
            jnp.max(here, axis=1, keepdims=True), jnp.max(before, axis=1, keepdims=True)
        )
        here = jnp.exp2(here - top).astype(jnp.bfloat16)
        before = jnp.exp2(before - top).astype(jnp.bfloat16)
        mixed = jnp.dot(here, late_v[...], preferred_element_type=jnp.float32)
        mixed += jnp.dot(before, early_v[...], preferred_element_type=jnp.float32)
        pack_result(mixed, packed_ref, i * QB, QB)
        return carry

    lax.fori_loop(0, 16 // QB, late_block, 0)
    pair = place_ref[2]
    scatter_halo(packed_ref, grid_ref, out_ref, place_ref[3], pair)
    copy = pltpu.make_async_copy(out_ref, out_hbm.at[pl.ds(8 - 8 * pair, 8)], sem)
    copy.start()

    def early_block(i, carry):
        query = recv_ref[pl.ds(early + i * QB, QB), :OWN, :].reshape(QB * OWN, HD)
        here = scores_of(query, early_k) * scale
        top = jnp.max(here, axis=1, keepdims=True)
        here = jnp.exp2(here - top).astype(jnp.bfloat16)
        mix_ref[pl.ds(i * QB * OWN, QB * OWN), :] = jnp.dot(
            here, early_v[...], preferred_element_type=jnp.float32
        )
        max_ref[pl.ds(i * QB * OWN, QB * OWN), :] = jnp.broadcast_to(top, (QB * OWN, HD))
        return carry

    lax.fori_loop(0, 16 // QB, early_block, 0)
    copy.wait()


def halo_scratch():
    return [
        pltpu.VMEM((16, OWN // 2, HD), jnp.float32),
        pltpu.VMEM((4, 2, 10, 8, HD), jnp.float32),
        pltpu.VMEM((8, 128, HD), jnp.bfloat16),
        pltpu.SemaphoreType.DMA,
    ]


def attend_here(place, recv):
    vmem = pl.BlockSpec(memory_space=pltpu.VMEM)
    tokens = 16 * OWN
    return pl.pallas_call(
        attend_here_kernel,
        out_shape=(
            pltpu.HBM((16, 128, HD), jnp.bfloat16),
            jax.ShapeDtypeStruct((tokens, HD), jnp.float32),
            jax.ShapeDtypeStruct((tokens, HD), jnp.float32),
        ),
        in_specs=[pl.BlockSpec(memory_space=pltpu.SMEM), vmem],
        out_specs=(pl.BlockSpec(memory_space=pltpu.HBM), vmem, vmem),
        scratch_shapes=[pltpu.VMEM((tokens, HD), jnp.bfloat16)] * 2 + halo_scratch(),
        compiler_params=pltpu.CompilerParams(vmem_limit_bytes=VMEM_BYTES),
        cost_estimate=pl.CostEstimate(
            flops=4 * 3 * tokens * tokens * HD, bytes_accessed=4 << 20, transcendentals=3 * tokens * tokens
        ),
    )(place, recv)


def attend_prior_kernel(
    place_ref, recv_ref, prior_ref, max_ref, mix_ref, late_hbm, out_hbm, prior_v, packed_ref, grid_ref,
    out_ref, sem,
):
    early = place_ref[0]
    penalty = jnp.where(place_ref[1] > 0, 0.0, -1e30).astype(jnp.float32)
    spread_values(prior_ref[:, OWN:, :], prior_v)
    prior_k = prior_ref[:, :OWN, :].reshape(16 * OWN, HD)
    scale = fold_scale()

    blocks = range(16 // PB)
    scores = []
    for i in blocks:
        query = recv_ref[pl.ds(early + i * PB, PB), :OWN, :].reshape(PB * OWN, HD)
        scores.append(scores_of(query, prior_k) * scale + penalty)
    for i in blocks:
        rows = pl.ds(i * PB * OWN, PB * OWN)
        old = max_ref[rows, :]
        top = jnp.maximum(old[:, :1], jnp.max(scores[i], axis=1, keepdims=True))
        before = jnp.exp2(scores[i] - top).astype(jnp.bfloat16)
        mixed = jnp.dot(before, prior_v[...], preferred_element_type=jnp.float32)
        mixed += mix_ref[rows, :] * jnp.exp2(old - top)
        pack_result(mixed, packed_ref, i * PB, PB)
    scatter_halo(packed_ref, grid_ref, out_ref, place_ref[3], 0)
    copy = pltpu.make_async_copy(out_ref, out_hbm.at[pl.ds(8 * place_ref[2], 8)], sem)
    copy.start()
    copy.wait()


def scatter_halo(packed_ref, grid_ref, out_ref, high, flip):
    grid_ref[...] = jnp.zeros_like(grid_ref)
    for b in range(2):
        tile_high = b + flip * (1 - 2 * b)
        for core in range(2):
            row = 2 * (2 * tile_high + core) + 1
            for x in range(4):
                block = x * 4 + b * 2 + core
                for frame in range(2):
                    for sub in range(2):
                        line = packed_ref[block, pl.ds(frame * 12 + sub, 6, stride=2), :]
                        grid_ref[x, frame, row + sub, 1:7, :] = line
                        if x < 3:
                            grid_ref[x + 1, frame, row + sub, 0:1, :] = line[5:6]
                        if x > 0:
                            grid_ref[x - 1, frame, row + sub, 7:8, :] = line[0:1]
    for x in range(4):
        for core in range(2):
            for part in range(2):
                row = 2 * (2 * (high if part == 0 else 1 - high) + core)
                tile = grid_ref[x, :, pl.ds(row, 4), :, :].reshape(64, HD)
                out_ref[x * 2 + core, part * 64 : (part + 1) * 64, :] = tile.astype(jnp.bfloat16)


def attend_prior(place, recv, prior, top, mix, sent):
    vmem = pl.BlockSpec(memory_space=pltpu.VMEM)
    hbm = pl.BlockSpec(memory_space=pltpu.HBM)
    tokens = 16 * OWN
    return pl.pallas_call(
        attend_prior_kernel,
        out_shape=pltpu.HBM((16, 128, HD), jnp.bfloat16),
        in_specs=[pl.BlockSpec(memory_space=pltpu.SMEM)] + [vmem] * 4 + [hbm],
        out_specs=hbm,
        input_output_aliases={5: 0},
        scratch_shapes=[pltpu.VMEM((tokens, HD), jnp.bfloat16)] + halo_scratch(),
        compiler_params=pltpu.CompilerParams(vmem_limit_bytes=VMEM_BYTES),
    )(place, recv, prior, top, mix, sent)


def sum_kernel(level_ref, back_ref, noisy_ref, own_ref, own_sent_ref, other_ref):
    total = back_ref[0].astype(jnp.float32)
    for k in range(1, 16):
        total += back_ref[k].astype(jnp.float32)
    own = noisy_ref[...] - level_ref[0] * total[:64]
    own_ref[...] = own
    own_sent_ref[...] = own.astype(jnp.bfloat16)
    other_ref[...] = (-level_ref[0] * total[64:]).astype(jnp.bfloat16)


def sum_heads(level, back, noisy):
    vmem = pl.BlockSpec(memory_space=pltpu.VMEM)
    return pl.pallas_call(
        sum_kernel,
        out_shape=(
            jax.ShapeDtypeStruct((64, HD), jnp.float32),
            jax.ShapeDtypeStruct((64, HD), jnp.bfloat16),
            jax.ShapeDtypeStruct((64, HD), jnp.bfloat16),
        ),
        in_specs=[pl.BlockSpec(memory_space=pltpu.SMEM), vmem, vmem],
        out_specs=(vmem, vmem, vmem),
        compiler_params=pltpu.CompilerParams(vmem_limit_bytes=4 * 1024 * 1024),
    )(level, back, noisy)


CH = 384
OC = 192
TAPS = {(0, 0): (0, 1), (0, 1): (2,), (1, 0): (0,), (1, 1): (1, 2)}


def spread_inlet(inlet_ref, wide_ref):
    blank = jnp.zeros((ZC, CH), jnp.bfloat16)
    for frame in range(3):
        for u in range(4):
            for v in range(4):
                row = frame * 256 + (u // 2 * 2 + v // 2) * LAT + (u % 2 * 2 + v % 2) * ZC
                for sub in range(4):
                    b, e = u - sub // 2, v - sub % 2
                    tap = blank
                    if 0 <= b < 3 and 0 <= e < 3:
                        first = ((frame * 3 + b) * 3 + e) * ZC
                        tap = inlet_ref[first : first + ZC, :]
                    wide_ref[row : row + ZC, sub * CH : (sub + 1) * CH] = tap


def ready_kernel(inlet_ref, time_hbm, window_hbm, order_ref, wide_ref, time_ref, window_ref, sems):
    copies = (
        pltpu.make_async_copy(time_hbm, time_ref, sems.at[0]),
        pltpu.make_async_copy(window_hbm, window_ref, sems.at[1]),
    )
    for copy in copies:
        copy.start()
    spread_inlet(inlet_ref, wide_ref)
    for copy in copies:
        copy.wait()


def ready_weights(inlet, time_weight, window, order):
    vmem = pl.BlockSpec(memory_space=pltpu.VMEM)
    hbm = pl.BlockSpec(memory_space=pltpu.HBM)
    return pl.pallas_call(
        ready_kernel,
        out_shape=(
            pltpu.VMEM((768, 4 * CH), jnp.bfloat16),
            pltpu.VMEM((3 * CH, 2 * CH), jnp.bfloat16),
            pltpu.VMEM((4 * CH, 4 * OC), jnp.bfloat16),
        ),
        in_specs=[vmem, hbm, hbm, pl.BlockSpec(memory_space=pl.ANY)],
        out_specs=(vmem, vmem, vmem),
        scratch_shapes=[pltpu.SemaphoreType.DMA((2,))],
        compiler_params=pltpu.CompilerParams(vmem_limit_bytes=12 * 1024 * 1024),
        cost_estimate=pl.CostEstimate(flops=4 << 20, bytes_accessed=8 << 20, transcendentals=0),
    )(
        inlet,
        pltpu.with_memory_space_constraint(time_weight, pltpu.HBM),
        pltpu.with_memory_space_constraint(window, pltpu.HBM),
        order,
    )


def window_kernel(spatial_ref, window_ref):
    for wy in range(2):
        for wx in range(2):
            rows = slice((2 * wy + wx) * CH, (2 * wy + wx + 1) * CH)
            rest = []
            for oy in range(2):
                for ox in range(2):
                    total = None
                    for b in TAPS[oy, wy]:
                        for e in TAPS[ox, wx]:
                            tap = spatial_ref[b, e].astype(jnp.float32)
                            total = tap if total is None else total + tap
                    out = 2 * oy + ox
                    window_ref[rows, out * 128 : (out + 1) * 128] = total[:, :128].astype(jnp.bfloat16)
                    rest.append(total[:, 128:])
            for oy in range(2):
                both = jnp.concatenate([rest[2 * oy], rest[2 * oy + 1]], axis=1)
                window_ref[rows, (4 + oy) * 128 : (5 + oy) * 128] = both.astype(jnp.bfloat16)


def window_weights(spatial_weight):
    vmem = pl.BlockSpec(memory_space=pltpu.VMEM)
    return pl.pallas_call(
        window_kernel,
        out_shape=jax.ShapeDtypeStruct((4 * CH, 4 * OC), jnp.bfloat16),
        in_specs=[vmem],
        out_specs=vmem,
        compiler_params=pltpu.CompilerParams(vmem_limit_bytes=16 * 1024 * 1024),
        cost_estimate=pl.CostEstimate(flops=4 << 20, bytes_accessed=4 << 20, transcendentals=0),
    )(spatial_weight)


SPACE_START = (0, 96, 192, 256)
WIN = 24


def decode_kernel(
    place_ref, before_own_ref, before_other_ref, own_ref, other_ref, wide_ref, inlet_bias_ref, time_ref, time_bias_ref, window_ref,
    space_bias_ref, out_hbm, patch_ref, feature_ref, time_in_ref, double_ref, shift_ref, space_in_ref,
    low_ref, rest_ref, out_ref, sems,
):
    has_prior, tile, head = place_ref[0], place_ref[1], place_ref[2]
    for half, (one_ref, two_ref) in enumerate(((before_own_ref, before_other_ref), (own_ref, other_ref))):
        cells = one_ref[...].astype(jnp.float32) + two_ref[...].astype(jnp.float32)
        cells = cells.astype(jnp.bfloat16).astype(jnp.float32)
        after = jnp.concatenate([cells[1:], cells[:1]], axis=0)
        for part in range(2):
            lanes = slice(part * LAT, (part + 1) * LAT)
            pairs = jnp.concatenate([cells[:, lanes], after[:, lanes]], axis=1)
            for frame in range(2):
                row = (half * 4 + part * 2 + frame) * WIN
                patch_ref[row : row + WIN, :128] = pairs[frame * 32 : frame * 32 + WIN]
                patch_ref[row : row + WIN, 128:] = pairs[frame * 32 + 8 : frame * 32 + 8 + WIN]
    taps = [patch_ref[a * WIN : (a + 6) * WIN, :].astype(jnp.bfloat16) for a in range(3)]
    features = jnp.dot(
        jnp.concatenate(taps, axis=1), wide_ref[...], preferred_element_type=jnp.float32
    )
    frame_row = lax.broadcasted_iota(jnp.int32, (6 * WIN, 1), 0)
    keep = jnp.logical_or(frame_row >= 2 * WIN, has_prior > 0)
    for sub in range(4):
        lanes = slice(sub * CH, (sub + 1) * CH)
        value = jnp.where(keep, features[:, lanes] + inlet_bias_ref[...], 0.0)
        feature_ref[:, lanes] = value
    for sub in range(4):
        for a in range(3):
            time_in_ref[sub * 96 : (sub + 1) * 96, a * CH : (a + 1) * CH] = feature_ref[
                a * WIN : a * WIN + 96, sub * CH : (sub + 1) * CH
            ].astype(jnp.bfloat16)
    doubled = jnp.dot(time_in_ref[...], time_ref[...], preferred_element_type=jnp.float32)
    place = lax.broadcasted_iota(jnp.int32, (96, 1), 0)
    window_row = lax.rem(place, WIN) // 8
    window_col = lax.rem(place, 8)
    for sub in range(4):
        row = 4 * tile + 2 * window_row - 1 + sub // 2
        col = 12 * head + 2 * window_col - 1 + sub % 2
        inside = jnp.logical_and(
            jnp.logical_and(row >= 0, row < 16), jnp.logical_and(col >= 0, col < 48)
        )
        value = jnp.where(inside, doubled[sub * 96 : (sub + 1) * 96] + time_bias_ref[...], 0.0)
        double_ref[sub, :96, :] = value
        double_ref[sub, 96:, :] = jnp.zeros((16, 2 * CH), jnp.float32)
        if sub % 2 == 0:
            shift_ref[sub // 2, :103, :] = double_ref[sub, 1:104, :]
            shift_ref[sub // 2, 103:, :] = jnp.zeros((9, 2 * CH), jnp.float32)
    low_bias = space_bias_ref[:, :128]
    rest_bias = space_bias_ref[:, 128:]
    copies = []
    for half in range(2):
        for py in range(2):
            for px in range(2):
                start = SPACE_START[2 * py + px]
                for wy in range(2):
                    for wx in range(2):
                        alpha, beta = (py + wy) % 2, (px + wx) % 2
                        ref = shift_ref.at[alpha] if px + wx == 2 else double_ref.at[2 * alpha + beta]
                        piece = slice((2 * wy + wx) * CH, (2 * wy + wx + 1) * CH)
                        for u in range(2):
                            lanes = slice(u * CH, (u + 1) * CH)
                            if py == 0:
                                spans = [(half * 2 * WIN, start + u * 2 * WIN, 2 * WIN)]
                            else:
                                spans = [
                                    ((half * 2 + t) * WIN + wy * 8, start + (u * 2 + t) * 16, 16)
                                    for t in range(2)
                                ]
                            for source, target, rows in spans:
                                space_in_ref[half, target : target + rows, piece] = ref[
                                    source : source + rows, lanes
                                ].astype(jnp.bfloat16)
        mixed = jnp.dot(space_in_ref[half], window_ref[...], preferred_element_type=jnp.float32)
        for py in range(2):
            for px in range(2):
                for oy in range(2):
                    for ox in range(2):
                        column = 8 - 1 + 2 * px + ox
                        out = 2 * oy + ox
                        for ri in range(3 - py):
                            high = 4 * ri - 1 + 2 * py + oy
                            if not 0 <= high < 8:
                                continue
                            for u in range(2):
                                for t in range(2):
                                    row = SPACE_START[2 * py + px] + ri * 8
                                    row += (u * 2 + t) * (WIN if py == 0 else 16)
                                    low = mixed[row : row + 8, out * 128 : (out + 1) * 128]
                                    rest = mixed[row : row + 8, (4 + oy) * 128 : (5 + oy) * 128]
                                    if ox:
                                        rest = pltpu.roll(rest, 64, 1)
                                    spot = pl.ds(column, 8, stride=4)
                                    line = (2 * (half * 2 + t) + u) * 8 + high
                                    low_ref[line, spot, :] = low
                                    rest_ref[line, spot, :] = rest
        for frame in range(half * 4, half * 4 + 4):
            for high in range(8):
                line = frame * 8 + high
                out_ref[frame, high, :, :128] = (low_ref[line, 8:32, :] + low_bias).astype(
                    jnp.bfloat16
                )
                out_ref[frame, high, :, 128:] = (rest_ref[line, 8:32, :LAT] + rest_bias).astype(
                    jnp.bfloat16
                )
        frames = pl.ds(half * 4, 4)
        copy = pltpu.make_async_copy(out_ref.at[frames], out_hbm.at[frames], sems.at[half])
        copy.start()
        copies.append(copy)
    for copy in copies:
        copy.wait()


def decode(place, before_own, before_other, own, other, wide, inlet_bias, time_weight, time_bias, window, space_bias):
    vmem = pl.BlockSpec(memory_space=pltpu.VMEM)
    hbm = pl.BlockSpec(memory_space=pltpu.HBM)
    f32, bf16 = jnp.float32, jnp.bfloat16
    wide, time_weight, window = (
        pltpu.with_memory_space_constraint(weight, pltpu.VMEM) for weight in (wide, time_weight, window)
    )
    return pl.pallas_call(
        decode_kernel,
        out_shape=pltpu.HBM((8, 8, 24, OC), bf16),
        in_specs=[pl.BlockSpec(memory_space=pltpu.SMEM)] + [vmem] * 10,
        out_specs=hbm,
        scratch_shapes=[
            pltpu.VMEM((8 * WIN, 256), f32),
            pltpu.VMEM((6 * WIN, 4 * CH), f32),
            pltpu.VMEM((384, 3 * CH), bf16),
            pltpu.VMEM((4, 112, 2 * CH), f32),
            pltpu.VMEM((2, 112, 2 * CH), f32),
            pltpu.VMEM((2, 320, 4 * CH), bf16),
            pltpu.VMEM((64, 40, 128), f32),
            pltpu.VMEM((64, 40, 128), f32),
            pltpu.VMEM((8, 8, 24, OC), bf16),
            pltpu.SemaphoreType.DMA((2,)),
        ],
        compiler_params=pltpu.CompilerParams(vmem_limit_bytes=VMEM_BYTES),
    )(place, before_own, before_other, own, other, wide, inlet_bias, time_weight, time_bias, window, space_bias)


def with_halo(cells, sides, width):
    for axis, dim in sides:
        count = lax.axis_size(axis)
        ends = count - 1
        head = lax.slice_in_dim(cells, 0, width, axis=dim)
        tail = lax.slice_in_dim(cells, cells.shape[dim] - width, cells.shape[dim], axis=dim)
        cells = jnp.concatenate(
            [
                lax.ppermute(tail, axis, [(i, (i + 1) % count) for i in range(ends)]),
                cells,
                lax.ppermute(head, axis, [((i + 1) % count, i) for i in range(ends)]),
            ],
            axis=dim,
        )
    return cells


def shards(
    query_states,
    key_states,
    value_states,
    noisy_latent,
    noise_level,
    head_weight,
    inlet_weight,
    inlet_bias,
    temporal_weight,
    temporal_bias,
    spatial_weight,
    spatial_bias,
):
    groups = pair_groups()
    grp = lax.axis_index("grp")
    pair = (grp // 2) % 2
    has_prior = grp > 0
    early = 16 * pair
    pair_has_prior = (grp // 2 > 0).astype(jnp.int32)
    high = lax.axis_index("tile") // 2
    place = jnp.stack([early, pair_has_prior, pair, high]).astype(jnp.int32)
    sent = prep(query_states, key_states, value_states, head_weight)
    sent, spatial_weight, noisy_latent = lax.optimization_barrier(
        (sent, spatial_weight, noisy_latent)
    )
    window = window_weights(spatial_weight)
    halo_noisy = with_halo(noisy_latent[0], (("head", 2), ("tile", 1)), 1)
    halo_noisy = halo_noisy.reshape(2, 2, 4, 8, LAT).transpose(1, 2, 3, 0, 4).reshape(64, HD)
    recv = lax.all_to_all(sent, AXES, 0, 0, tiled=True, axis_index_groups=groups)
    late_kv = late_part(place, recv, (halo_noisy, window))
    prior = lax.ppermute(late_kv, AXES, prior_route(groups))
    partial, top, mix = attend_here(place, recv)
    partial = attend_prior(place, recv, prior, top, mix, partial)
    back = lax.all_to_all(partial, AXES, 0, 0, tiled=True, axis_index_groups=half_groups(groups))
    own, own_sent, other_sent = sum_heads(noise_level, back, halo_noisy)
    across = lax.ppermute(other_sent, "tile", ACROSS)
    before_own = lax.ppermute(own_sent, AXES, span_route(0))
    before_other = lax.ppermute(other_sent, AXES, span_route(2))
    clean = own + across.astype(jnp.float32)
    clean_latent = clean.reshape(2, 4, 8, 2, LAT)[:, 1:3, 1:7].transpose(3, 0, 1, 2, 4)
    clean_latent = clean_latent.reshape(noisy_latent.shape)
    wide, time_ready, window = ready_weights(
        inlet_weight.reshape(27 * ZC, CH), temporal_weight.reshape(3 * CH, 2 * CH), window, clean_latent
    )
    where = jnp.stack([has_prior.astype(jnp.int32), lax.axis_index("tile"), lax.axis_index("head")])
    decoded = decode(
        where,
        before_own,
        before_other,
        own,
        across,
        wide,
        inlet_bias[None],
        time_ready,
        temporal_bias[None],
        window,
        spatial_bias[None],
    )
    return (clean_latent, decoded[None])


def solution(mesh):
    return jax.shard_map(
        shards,
        mesh=mesh,
        in_specs=(
            P("grp", None, "tile", "head", None),
            P("grp", None, "tile", "head", None),
            P("grp", None, "tile", "head", None),
            P("grp", None, "tile", "head", None),
            P("grp"),
            P(),
            P(),
            P(),
            P(),
            P(),
            P(),
            P(),
        ),
        out_specs=(P("grp", None, "tile", "head", None), P("grp", None, "tile", "head", None)),
        check_vma=False,
    )
```

```python
import math

import jax
import jax.numpy as jnp
from jax import lax
from jax.experimental import pallas as pl
from jax.experimental.pallas import tpu as pltpu
from jax.sharding import PartitionSpec as P

HD = 128
ZC = 16
HEADS = 32
OWN = 48
LAT = 64
ROWS = 2 * OWN + OWN // 2
AXES = ("grp", "head", "tile")
VMEM_BYTES = 32 * 1024 * 1024


def device_id(y, pair, low, x, high, core):
    return ((y * 4 + 2 * pair + low) * 4 + x) * 4 + 2 * high + core


def pair_groups():
    groups = []
    for y in range(4):
        for pair in range(2):
            members = []
            for a in range(2):
                for x in range(4):
                    for b in range(2):
                        for core in range(2):
                            low = a if pair == 0 else 1 - a
                            high = b if pair == 0 or a == 1 else 1 - b
                            members.append(device_id(y, pair, low, x, high, core))
            groups.append(members)
    return groups


def half_groups(groups):
    return [[d for d in group if d // 2 % 2 == high] for group in groups for high in range(2)]


ACROSS = [(0, 2), (1, 3), (2, 0), (3, 1)]


def span_route(turn):
    return [
        ((span * 4 + x) * 4 + tile, ((span + 1) * 4 + x) * 4 + (tile + turn) % 4)
        for span in range(15)
        for x in range(4)
        for tile in range(4)
    ]


def prior_route(groups):
    return [(groups[g][k], groups[g + 1][k]) for g in range(len(groups) - 1) for k in range(HEADS)]


PREP_STEPS = 2
PREP_HEADS = HEADS // PREP_STEPS


def prep_kernel(query_ref, key_ref, value_ref, weight_ref, out_ref):
    dims = (((1,), (1,)), ((), ()))
    width = PREP_HEADS * HD
    query = query_ref[0].reshape(OWN, width)
    key = key_ref[0].reshape(OWN, width)
    value = value_ref[0].reshape(OWN, width)
    for h in range(PREP_HEADS):
        lanes = slice(h * HD, (h + 1) * HD)
        out_ref[h, 0:OWN, :] = query[:, lanes]
        out_ref[h, OWN : 2 * OWN, :] = key[:, lanes]
        folded = lax.dot_general(
            value[:, lanes], weight_ref[:, lanes], dims, preferred_element_type=jnp.float32
        )
        packed = jnp.concatenate([folded[: OWN // 2], folded[OWN // 2 :]], axis=1)
        out_ref[h, 2 * OWN : ROWS, :] = packed.astype(jnp.bfloat16)


def own_order(states):
    return pltpu.with_memory_space_constraint(states.transpose(0, 1, 3, 2, 4), pltpu.HBM)


def prep(query, key, value, weight):
    width = PREP_HEADS * HD
    tile = pl.BlockSpec((1, 4, 6, 2, width), lambda i: (0, 0, 0, 0, i))
    return pl.pallas_call(
        prep_kernel,
        grid=(PREP_STEPS,),
        out_shape=jax.ShapeDtypeStruct((HEADS, ROWS, HD), jnp.bfloat16),
        in_specs=[tile, tile, tile, pl.BlockSpec((LAT, width), lambda i: (0, i))],
        out_specs=pl.BlockSpec((PREP_HEADS, ROWS, HD), lambda i: (i, 0, 0)),
        compiler_params=pltpu.CompilerParams(vmem_limit_bytes=16 * 1024 * 1024),
    )(own_order(query), own_order(key), own_order(value), pltpu.with_memory_space_constraint(weight.T, pltpu.HBM))


def spread_values(packed, target):
    lower = packed[:, :, :LAT].astype(jnp.float32)
    upper = packed[:, :, LAT:].astype(jnp.float32)
    both = jnp.concatenate([lower, upper], axis=1).reshape(16 * OWN, LAT)
    ones = jnp.ones((16 * OWN, HD - LAT), jnp.float32)
    target[...] = jnp.concatenate([both, ones], axis=1).astype(jnp.bfloat16)


def fold_scale():
    return (1.0 / math.sqrt(HD)) * math.log2(math.e)


def scores_of(query, keys):
    dims = (((1,), (1,)), ((), ()))
    return lax.dot_general(query, keys, dims, preferred_element_type=jnp.float32)


def pack_result(mixed, out_ref, start, blocks):
    velocity = mixed[:, :LAT] / mixed[:, LAT : 2 * LAT]
    velocity = velocity.reshape(blocks, OWN, LAT)
    packed = jnp.concatenate([velocity[:, : OWN // 2], velocity[:, OWN // 2 :]], axis=2)
    out_ref[pl.ds(start, blocks)] = packed.astype(out_ref.dtype)


QB = 16
PB = 8


def late_part_kernel(place_ref, recv_ref, *rest):
    rest[-1][...] = recv_ref[pl.ds(16 - place_ref[0], 16), OWN:, :]


def late_part(place, recv, ready):
    vmem = pl.BlockSpec(memory_space=pltpu.VMEM)
    return pl.pallas_call(
        late_part_kernel,
        out_shape=jax.ShapeDtypeStruct((16, ROWS - OWN, HD), jnp.bfloat16),
        in_specs=[pl.BlockSpec(memory_space=pltpu.SMEM), vmem]
        + [pl.BlockSpec(memory_space=pl.ANY)] * len(ready),
        out_specs=vmem,
        compiler_params=pltpu.CompilerParams(vmem_limit_bytes=4 * 1024 * 1024),
    )(place, recv, *ready)


def attend_here_kernel(
    place_ref, recv_ref, out_hbm, max_ref, mix_ref, early_v, late_v, packed_ref, grid_ref, out_ref, sem
):
    early = place_ref[0]
    late = 16 - early
    spread_values(recv_ref[pl.ds(early, 16), 2 * OWN :, :], early_v)
    spread_values(recv_ref[pl.ds(late, 16), 2 * OWN :, :], late_v)
    early_k = recv_ref[pl.ds(early, 16), OWN : 2 * OWN, :].reshape(16 * OWN, HD)
    late_k = recv_ref[pl.ds(late, 16), OWN : 2 * OWN, :].reshape(16 * OWN, HD)
    scale = fold_scale()

    def late_block(i, carry):
        query = recv_ref[pl.ds(late + i * QB, QB), :OWN, :].reshape(QB * OWN, HD)
        here = scores_of(query, late_k) * scale
        before = scores_of(query, early_k) * scale
        top = jnp.maximum(
            jnp.max(here, axis=1, keepdims=True), jnp.max(before, axis=1, keepdims=True)
        )
        here = jnp.exp2(here - top).astype(jnp.bfloat16)
        before = jnp.exp2(before - top).astype(jnp.bfloat16)
        mixed = jnp.dot(here, late_v[...], preferred_element_type=jnp.float32)
        mixed += jnp.dot(before, early_v[...], preferred_element_type=jnp.float32)
        pack_result(mixed, packed_ref, i * QB, QB)
        return carry

    lax.fori_loop(0, 16 // QB, late_block, 0)
    pair = place_ref[2]
    scatter_halo(packed_ref, grid_ref, out_ref, place_ref[3], pair)
    copy = pltpu.make_async_copy(out_ref, out_hbm.at[pl.ds(8 - 8 * pair, 8)], sem)
    copy.start()

    def early_block(i, carry):
        query = recv_ref[pl.ds(early + i * QB, QB), :OWN, :].reshape(QB * OWN, HD)
        here = scores_of(query, early_k) * scale
        top = jnp.max(here, axis=1, keepdims=True)
        here = jnp.exp2(here - top).astype(jnp.bfloat16)
        mix_ref[pl.ds(i * QB * OWN, QB * OWN), :] = jnp.dot(
            here, early_v[...], preferred_element_type=jnp.float32
        )
        max_ref[pl.ds(i * QB * OWN, QB * OWN), :] = jnp.broadcast_to(top, (QB * OWN, HD))
        return carry

    lax.fori_loop(0, 16 // QB, early_block, 0)
    copy.wait()


def halo_scratch():
    return [
        pltpu.VMEM((16, OWN // 2, HD), jnp.float32),
        pltpu.VMEM((4, 2, 10, 8, HD), jnp.float32),
        pltpu.VMEM((8, 128, HD), jnp.bfloat16),
        pltpu.SemaphoreType.DMA,
    ]


def attend_here(place, recv):
    vmem = pl.BlockSpec(memory_space=pltpu.VMEM)
    tokens = 16 * OWN
    return pl.pallas_call(
        attend_here_kernel,
        out_shape=(
            pltpu.HBM((16, 128, HD), jnp.bfloat16),
            jax.ShapeDtypeStruct((tokens, HD), jnp.float32),
            jax.ShapeDtypeStruct((tokens, HD), jnp.float32),
        ),
        in_specs=[pl.BlockSpec(memory_space=pltpu.SMEM), vmem],
        out_specs=(pl.BlockSpec(memory_space=pltpu.HBM), vmem, vmem),
        scratch_shapes=[pltpu.VMEM((tokens, HD), jnp.bfloat16)] * 2 + halo_scratch(),
        compiler_params=pltpu.CompilerParams(vmem_limit_bytes=VMEM_BYTES),
        cost_estimate=pl.CostEstimate(
            flops=4 * 3 * tokens * tokens * HD, bytes_accessed=4 << 20, transcendentals=3 * tokens * tokens
        ),
    )(place, recv)


def attend_prior_kernel(
    place_ref, recv_ref, prior_ref, max_ref, mix_ref, late_hbm, out_hbm, prior_v, packed_ref, grid_ref,
    out_ref, sem,
):
    early = place_ref[0]
    penalty = jnp.where(place_ref[1] > 0, 0.0, -1e30).astype(jnp.float32)
    spread_values(prior_ref[:, OWN:, :], prior_v)
    prior_k = prior_ref[:, :OWN, :].reshape(16 * OWN, HD)
    scale = fold_scale()

    def block(i, carry):
        rows = pl.ds(i * PB * OWN, PB * OWN)
        query = recv_ref[pl.ds(early + i * PB, PB), :OWN, :].reshape(PB * OWN, HD)
        before = scores_of(query, prior_k) * scale + penalty
        old = max_ref[rows, :]
        top = jnp.maximum(old[:, :1], jnp.max(before, axis=1, keepdims=True))
        before = jnp.exp2(before - top).astype(jnp.bfloat16)
        mixed = jnp.dot(before, prior_v[...], preferred_element_type=jnp.float32)
        mixed += mix_ref[rows, :] * jnp.exp2(old - top)
        pack_result(mixed, packed_ref, i * PB, PB)
        return carry

    lax.fori_loop(0, 16 // PB, block, 0, unroll=True)
    scatter_halo(packed_ref, grid_ref, out_ref, place_ref[3], 0)
    copy = pltpu.make_async_copy(out_ref, out_hbm.at[pl.ds(8 * place_ref[2], 8)], sem)
    copy.start()
    copy.wait()


def scatter_halo(packed_ref, grid_ref, out_ref, high, flip):
    grid_ref[...] = jnp.zeros_like(grid_ref)
    for b in range(2):
        tile_high = b + flip * (1 - 2 * b)
        for core in range(2):
            row = 2 * (2 * tile_high + core) + 1
            for x in range(4):
                block = x * 4 + b * 2 + core
                for frame in range(2):
                    for sub in range(2):
                        line = packed_ref[block, pl.ds(frame * 12 + sub, 6, stride=2), :]
                        grid_ref[x, frame, row + sub, 1:7, :] = line
                        if x < 3:
                            grid_ref[x + 1, frame, row + sub, 0:1, :] = line[5:6]
                        if x > 0:
                            grid_ref[x - 1, frame, row + sub, 7:8, :] = line[0:1]
    for x in range(4):
        for core in range(2):
            for part in range(2):
                row = 2 * (2 * (high if part == 0 else 1 - high) + core)
                tile = grid_ref[x, :, pl.ds(row, 4), :, :].reshape(64, HD)
                out_ref[x * 2 + core, part * 64 : (part + 1) * 64, :] = tile.astype(jnp.bfloat16)


def attend_prior(place, recv, prior, top, mix, sent):
    vmem = pl.BlockSpec(memory_space=pltpu.VMEM)
    hbm = pl.BlockSpec(memory_space=pltpu.HBM)
    tokens = 16 * OWN
    return pl.pallas_call(
        attend_prior_kernel,
        out_shape=pltpu.HBM((16, 128, HD), jnp.bfloat16),
        in_specs=[pl.BlockSpec(memory_space=pltpu.SMEM)] + [vmem] * 4 + [hbm],
        out_specs=hbm,
        input_output_aliases={5: 0},
        scratch_shapes=[pltpu.VMEM((tokens, HD), jnp.bfloat16)] + halo_scratch(),
        compiler_params=pltpu.CompilerParams(vmem_limit_bytes=VMEM_BYTES),
    )(place, recv, prior, top, mix, sent)


def sum_kernel(level_ref, back_ref, noisy_ref, own_ref, own_sent_ref, other_ref):
    total = back_ref[0].astype(jnp.float32)
    for k in range(1, 16):
        total += back_ref[k].astype(jnp.float32)
    own = noisy_ref[...] - level_ref[0] * total[:64]
    own_ref[...] = own
    own_sent_ref[...] = own.astype(jnp.bfloat16)
    other_ref[...] = (-level_ref[0] * total[64:]).astype(jnp.bfloat16)


def sum_heads(level, back, noisy):
    vmem = pl.BlockSpec(memory_space=pltpu.VMEM)
    return pl.pallas_call(
        sum_kernel,
        out_shape=(
            jax.ShapeDtypeStruct((64, HD), jnp.float32),
            jax.ShapeDtypeStruct((64, HD), jnp.bfloat16),
            jax.ShapeDtypeStruct((64, HD), jnp.bfloat16),
        ),
        in_specs=[pl.BlockSpec(memory_space=pltpu.SMEM), vmem, vmem],
        out_specs=(vmem, vmem, vmem),
        compiler_params=pltpu.CompilerParams(vmem_limit_bytes=4 * 1024 * 1024),
    )(level, back, noisy)


CH = 384
OC = 192
TAPS = {(0, 0): (0, 1), (0, 1): (2,), (1, 0): (0,), (1, 1): (1, 2)}


def spread_inlet(inlet_ref, wide_ref):
    blank = jnp.zeros((ZC, CH), jnp.bfloat16)
    for frame in range(3):
        for u in range(4):
            for v in range(4):
                row = frame * 256 + (u // 2 * 2 + v // 2) * LAT + (u % 2 * 2 + v % 2) * ZC
                for sub in range(4):
                    b, e = u - sub // 2, v - sub % 2
                    tap = blank
                    if 0 <= b < 3 and 0 <= e < 3:
                        first = ((frame * 3 + b) * 3 + e) * ZC
                        tap = inlet_ref[first : first + ZC, :]
                    wide_ref[row : row + ZC, sub * CH : (sub + 1) * CH] = tap


def ready_kernel(inlet_ref, time_hbm, window_hbm, order_ref, wide_ref, time_ref, window_ref, sems):
    copies = (
        pltpu.make_async_copy(time_hbm, time_ref, sems.at[0]),
        pltpu.make_async_copy(window_hbm, window_ref, sems.at[1]),
    )
    for copy in copies:
        copy.start()
    spread_inlet(inlet_ref, wide_ref)
    for copy in copies:
        copy.wait()


def ready_weights(inlet, time_weight, window, order):
    vmem = pl.BlockSpec(memory_space=pltpu.VMEM)
    hbm = pl.BlockSpec(memory_space=pltpu.HBM)
    return pl.pallas_call(
        ready_kernel,
        out_shape=(
            pltpu.VMEM((768, 4 * CH), jnp.bfloat16),
            pltpu.VMEM((3 * CH, 2 * CH), jnp.bfloat16),
            pltpu.VMEM((4 * CH, 4 * OC), jnp.bfloat16),
        ),
        in_specs=[vmem, hbm, hbm, pl.BlockSpec(memory_space=pl.ANY)],
        out_specs=(vmem, vmem, vmem),
        scratch_shapes=[pltpu.SemaphoreType.DMA((2,))],
        compiler_params=pltpu.CompilerParams(vmem_limit_bytes=12 * 1024 * 1024),
        cost_estimate=pl.CostEstimate(flops=4 << 20, bytes_accessed=8 << 20, transcendentals=0),
    )(
        inlet,
        pltpu.with_memory_space_constraint(time_weight, pltpu.HBM),
        pltpu.with_memory_space_constraint(window, pltpu.HBM),
        order,
    )


def window_kernel(spatial_ref, window_ref):
    for wy in range(2):
        for wx in range(2):
            rows = slice((2 * wy + wx) * CH, (2 * wy + wx + 1) * CH)
            rest = []
            for oy in range(2):
                for ox in range(2):
                    total = None
                    for b in TAPS[oy, wy]:
                        for e in TAPS[ox, wx]:
                            tap = spatial_ref[b, e].astype(jnp.float32)
                            total = tap if total is None else total + tap
                    out = 2 * oy + ox
                    window_ref[rows, out * 128 : (out + 1) * 128] = total[:, :128].astype(jnp.bfloat16)
                    rest.append(total[:, 128:])
            for oy in range(2):
                both = jnp.concatenate([rest[2 * oy], rest[2 * oy + 1]], axis=1)
                window_ref[rows, (4 + oy) * 128 : (5 + oy) * 128] = both.astype(jnp.bfloat16)


def window_weights(spatial_weight):
    vmem = pl.BlockSpec(memory_space=pltpu.VMEM)
    return pl.pallas_call(
        window_kernel,
        out_shape=jax.ShapeDtypeStruct((4 * CH, 4 * OC), jnp.bfloat16),
        in_specs=[vmem],
        out_specs=vmem,
        compiler_params=pltpu.CompilerParams(vmem_limit_bytes=16 * 1024 * 1024),
        cost_estimate=pl.CostEstimate(flops=4 << 20, bytes_accessed=4 << 20, transcendentals=0),
    )(spatial_weight)


SPACE_START = (0, 96, 192, 256)
WIN = 24


def decode_kernel(
    place_ref, before_own_ref, before_other_ref, own_ref, other_ref, wide_ref, inlet_bias_ref, time_ref, time_bias_ref, window_ref,
    space_bias_ref, out_hbm, patch_ref, feature_ref, time_in_ref, double_ref, shift_ref, space_in_ref,
    low_ref, rest_ref, out_ref, sems,
):
    has_prior, tile, head = place_ref[0], place_ref[1], place_ref[2]
    for half, (one_ref, two_ref) in enumerate(((before_own_ref, before_other_ref), (own_ref, other_ref))):
        cells = one_ref[...].astype(jnp.float32) + two_ref[...].astype(jnp.float32)
        cells = cells.astype(jnp.bfloat16).astype(jnp.float32)
        after = jnp.concatenate([cells[1:], cells[:1]], axis=0)
        for part in range(2):
            lanes = slice(part * LAT, (part + 1) * LAT)
            pairs = jnp.concatenate([cells[:, lanes], after[:, lanes]], axis=1)
            for frame in range(2):
                row = (half * 4 + part * 2 + frame) * WIN
                patch_ref[row : row + WIN, :128] = pairs[frame * 32 : frame * 32 + WIN]
                patch_ref[row : row + WIN, 128:] = pairs[frame * 32 + 8 : frame * 32 + 8 + WIN]
    taps = [patch_ref[a * WIN : (a + 6) * WIN, :].astype(jnp.bfloat16) for a in range(3)]
    features = jnp.dot(
        jnp.concatenate(taps, axis=1), wide_ref[...], preferred_element_type=jnp.float32
    )
    frame_row = lax.broadcasted_iota(jnp.int32, (6 * WIN, 1), 0)
    keep = jnp.logical_or(frame_row >= 2 * WIN, has_prior > 0)
    for sub in range(4):
        lanes = slice(sub * CH, (sub + 1) * CH)
        value = jnp.where(keep, features[:, lanes] + inlet_bias_ref[...], 0.0)
        feature_ref[:, lanes] = value
    for sub in range(4):
        for a in range(3):
            time_in_ref[sub * 96 : (sub + 1) * 96, a * CH : (a + 1) * CH] = feature_ref[
                a * WIN : a * WIN + 96, sub * CH : (sub + 1) * CH
            ].astype(jnp.bfloat16)
    doubled = jnp.dot(time_in_ref[...], time_ref[...], preferred_element_type=jnp.float32)
    place = lax.broadcasted_iota(jnp.int32, (96, 1), 0)
    window_row = lax.rem(place, WIN) // 8
    window_col = lax.rem(place, 8)
    for sub in range(4):
        row = 4 * tile + 2 * window_row - 1 + sub // 2
        col = 12 * head + 2 * window_col - 1 + sub % 2
        inside = jnp.logical_and(
            jnp.logical_and(row >= 0, row < 16), jnp.logical_and(col >= 0, col < 48)
        )
        value = jnp.where(inside, doubled[sub * 96 : (sub + 1) * 96] + time_bias_ref[...], 0.0)
        double_ref[sub, :96, :] = value
        double_ref[sub, 96:, :] = jnp.zeros((16, 2 * CH), jnp.float32)
        if sub % 2 == 0:
            shift_ref[sub // 2, :103, :] = double_ref[sub, 1:104, :]
            shift_ref[sub // 2, 103:, :] = jnp.zeros((9, 2 * CH), jnp.float32)
    low_bias = space_bias_ref[:, :128]
    rest_bias = space_bias_ref[:, 128:]
    copies = []
    for half in range(2):
        for py in range(2):
            for px in range(2):
                start = SPACE_START[2 * py + px]
                for wy in range(2):
                    for wx in range(2):
                        alpha, beta = (py + wy) % 2, (px + wx) % 2
                        ref = shift_ref.at[alpha] if px + wx == 2 else double_ref.at[2 * alpha + beta]
                        piece = slice((2 * wy + wx) * CH, (2 * wy + wx + 1) * CH)
                        for u in range(2):
                            lanes = slice(u * CH, (u + 1) * CH)
                            if py == 0:
                                spans = [(half * 2 * WIN, start + u * 2 * WIN, 2 * WIN)]
                            else:
                                spans = [
                                    ((half * 2 + t) * WIN + wy * 8, start + (u * 2 + t) * 16, 16)
                                    for t in range(2)
                                ]
                            for source, target, rows in spans:
                                space_in_ref[half, target : target + rows, piece] = ref[
                                    source : source + rows, lanes
                                ].astype(jnp.bfloat16)
        mixed = jnp.dot(space_in_ref[half], window_ref[...], preferred_element_type=jnp.float32)
        for py in range(2):
            for px in range(2):
                for oy in range(2):
                    for ox in range(2):
                        column = 8 - 1 + 2 * px + ox
                        out = 2 * oy + ox
                        for ri in range(3 - py):
                            high = 4 * ri - 1 + 2 * py + oy
                            if not 0 <= high < 8:
                                continue
                            for u in range(2):
                                for t in range(2):
                                    row = SPACE_START[2 * py + px] + ri * 8
                                    row += (u * 2 + t) * (WIN if py == 0 else 16)
                                    low = mixed[row : row + 8, out * 128 : (out + 1) * 128]
                                    rest = mixed[row : row + 8, (4 + oy) * 128 : (5 + oy) * 128]
                                    if ox:
                                        rest = pltpu.roll(rest, 64, 1)
                                    spot = pl.ds(column, 8, stride=4)
                                    line = (2 * (half * 2 + t) + u) * 8 + high
                                    low_ref[line, spot, :] = low
                                    rest_ref[line, spot, :] = rest
        for frame in range(half * 4, half * 4 + 4):
            for high in range(8):
                line = frame * 8 + high
                out_ref[frame, high, :, :128] = (low_ref[line, 8:32, :] + low_bias).astype(
                    jnp.bfloat16
                )
                out_ref[frame, high, :, 128:] = (rest_ref[line, 8:32, :LAT] + rest_bias).astype(
                    jnp.bfloat16
                )
            copy = pltpu.make_async_copy(out_ref.at[frame], out_hbm.at[frame], sems.at[frame])
            copy.start()
            copies.append(copy)
    for copy in copies:
        copy.wait()


def decode(place, before_own, before_other, own, other, wide, inlet_bias, time_weight, time_bias, window, space_bias):
    vmem = pl.BlockSpec(memory_space=pltpu.VMEM)
    hbm = pl.BlockSpec(memory_space=pltpu.HBM)
    f32, bf16 = jnp.float32, jnp.bfloat16
    wide, time_weight, window = (
        pltpu.with_memory_space_constraint(weight, pltpu.VMEM) for weight in (wide, time_weight, window)
    )
    return pl.pallas_call(
        decode_kernel,
        out_shape=pltpu.HBM((8, 8, 24, OC), bf16),
        in_specs=[pl.BlockSpec(memory_space=pltpu.SMEM)] + [vmem] * 10,
        out_specs=hbm,
        scratch_shapes=[
            pltpu.VMEM((8 * WIN, 256), f32),
            pltpu.VMEM((6 * WIN, 4 * CH), f32),
            pltpu.VMEM((384, 3 * CH), bf16),
            pltpu.VMEM((4, 112, 2 * CH), f32),
            pltpu.VMEM((2, 112, 2 * CH), f32),
            pltpu.VMEM((2, 320, 4 * CH), bf16),
            pltpu.VMEM((64, 40, 128), f32),
            pltpu.VMEM((64, 40, 128), f32),
            pltpu.VMEM((8, 8, 24, OC), bf16),
            pltpu.SemaphoreType.DMA((8,)),
        ],
        compiler_params=pltpu.CompilerParams(vmem_limit_bytes=VMEM_BYTES),
    )(place, before_own, before_other, own, other, wide, inlet_bias, time_weight, time_bias, window, space_bias)


def with_halo(cells, sides, width):
    for axis, dim in sides:
        count = lax.axis_size(axis)
        ends = count - 1
        head = lax.slice_in_dim(cells, 0, width, axis=dim)
        tail = lax.slice_in_dim(cells, cells.shape[dim] - width, cells.shape[dim], axis=dim)
        cells = jnp.concatenate(
            [
                lax.ppermute(tail, axis, [(i, (i + 1) % count) for i in range(ends)]),
                cells,
                lax.ppermute(head, axis, [((i + 1) % count, i) for i in range(ends)]),
            ],
            axis=dim,
        )
    return cells


def shards(
    query_states,
    key_states,
    value_states,
    noisy_latent,
    noise_level,
    head_weight,
    inlet_weight,
    inlet_bias,
    temporal_weight,
    temporal_bias,
    spatial_weight,
    spatial_bias,
):
    groups = pair_groups()
    grp = lax.axis_index("grp")
    pair = (grp // 2) % 2
    has_prior = grp > 0
    early = 16 * pair
    pair_has_prior = (grp // 2 > 0).astype(jnp.int32)
    high = lax.axis_index("tile") // 2
    place = jnp.stack([early, pair_has_prior, pair, high]).astype(jnp.int32)
    sent = prep(query_states, key_states, value_states, head_weight)
    sent, spatial_weight, noisy_latent = lax.optimization_barrier(
        (sent, spatial_weight, noisy_latent)
    )
    window = window_weights(spatial_weight)
    halo_noisy = with_halo(noisy_latent[0], (("head", 2), ("tile", 1)), 1)
    halo_noisy = halo_noisy.reshape(2, 2, 4, 8, LAT).transpose(1, 2, 3, 0, 4).reshape(64, HD)
    recv = lax.all_to_all(sent, AXES, 0, 0, tiled=True, axis_index_groups=groups)
    late_kv = late_part(place, recv, (halo_noisy, window))
    prior = lax.ppermute(late_kv, AXES, prior_route(groups))
    partial, top, mix = attend_here(place, recv)
    partial = attend_prior(place, recv, prior, top, mix, partial)
    back = lax.all_to_all(partial, AXES, 0, 0, tiled=True, axis_index_groups=half_groups(groups))
    own, own_sent, other_sent = sum_heads(noise_level, back, halo_noisy)
    across = lax.ppermute(other_sent, "tile", ACROSS)
    before_other = lax.ppermute(other_sent, AXES, span_route(2))
    before_own = lax.ppermute(own_sent, AXES, span_route(0))
    clean = own + across.astype(jnp.float32)
    clean_latent = clean.reshape(2, 4, 8, 2, LAT)[:, 1:3, 1:7].transpose(3, 0, 1, 2, 4)
    clean_latent = clean_latent.reshape(noisy_latent.shape)
    wide, time_ready, window = ready_weights(
        inlet_weight.reshape(27 * ZC, CH), temporal_weight.reshape(3 * CH, 2 * CH), window, clean_latent
    )
    where = jnp.stack([has_prior.astype(jnp.int32), lax.axis_index("tile"), lax.axis_index("head")])
    decoded = decode(
        where,
        before_own,
        before_other,
        own,
        across,
        wide,
        inlet_bias[None],
        time_ready,
        temporal_bias[None],
        window,
        spatial_bias[None],
    )
    return (clean_latent, decoded[None])


def solution(mesh):
    return jax.shard_map(
        shards,
        mesh=mesh,
        in_specs=(
            P("grp", None, "tile", "head", None),
            P("grp", None, "tile", "head", None),
            P("grp", None, "tile", "head", None),
            P("grp", None, "tile", "head", None),
            P("grp"),
            P(),
            P(),
            P(),
            P(),
            P(),
            P(),
            P(),
        ),
        out_specs=(P("grp", None, "tile", "head", None), P("grp", None, "tile", "head", None)),
        check_vma=False,
    )
```
